32 devices in a mesh: grp: 2 (over y), gy: 4 (over z), gx: 2 (over x), col: 2 (over core).
Axes of the slice: x: 2, y: 2, z: 4, core: 2. Of those that a mesh axis runs over, the one named last changes fastest.
Arguments:
- fine_in: float32 [32, 16, 16, 256], P('col', 'grp', 'gy', 'gx'), parts along dimension 1, may hold values from -6 to 6
- context_in: float32 [64, 4, 4, 64], P('col', 'grp', 'gy', 'gx'), parts along dimension 1, may hold values from -6 to 6
- weight_fine: float32 [3, 3, 3, 32, 32], P(None, None, None, None, 'col'), may hold values from -0.21875 to 0.21875
- weight_coarse: float32 [3, 3, 3, 64, 64], P(None, None, None, None, 'col'), may hold values from -0.15625 to 0.15625
- lift_weight: float32 [64, 32], P(None, 'col'), may hold values from -0.75 to 0.75
- lower_weight: float32 [32, 64], P(None, 'col'), may hold values from -1 to 1
- block_row: int32 [8, 2], P('grp'), parts along dimension 0, may hold values from 0 to 3
- tile_count: int32 [8, 2], P('grp'), parts along dimension 0, may hold values from 1 to 4
- fine_cotangent: float32 [32, 16, 16, 256], P('col', 'grp', 'gy', 'gx'), parts along dimension 1, may hold values from -6 to 6
- coarse_cotangent: float32 [64, 4, 4, 64], P('col', 'grp', 'gy', 'gx'), parts along dimension 1, may hold values from -6 to 6
Outputs:
- joined_fine: float32 [32, 16, 16, 256], P('col', 'grp', 'gy', 'gx'), parts along dimension 1
- joined_coarse: float32 [64, 4, 4, 64], P('col', 'grp', 'gy', 'gx'), parts along dimension 1
- fine_gradient: float32 [6, 3, 3, 32, 32], P('grp', None, None, None, 'col'), parts along dimension 0
- coarse_gradient: float32 [6, 3, 3, 64, 64], P('grp', None, None, None, 'col'), parts along dimension 0
- lift_gradient: float32 [128, 32], P('grp', 'col'), parts along dimension 0
- lower_gradient: float32 [64, 64], P('grp', 'col'), parts along dimension 0
The draws below stay inside these ranges and needn't reach their ends.
There are 2 independent parts, one for each index of `grp`. The reference program is written for one: setup_inputs(seed, part) draws one part's arguments, and reference() takes and returns one part's arrays. A program takes and returns all parts, laid end to end along the dimension named above; an argument that names none is the same for every part. Nothing has to cross between parts.
All inputs are finite; a program needn't handle non-finite values.
Results may differ from the reference program's by a relative error of at most 0.000093.
Values sent between devices are 32-bit elements; how exact they have to be, the bound alone decides.
A program may use at most 64 MiB of HBM per device.

```python
import jax
import jax.numpy as jnp
from jax import lax

CF = 32
CC = 64
RATIO = 4
BZ = 2
BY = 1
BX = 32
FZ = 8
TY = 4
TX = 2
NYF = 16
NXF = 256
NYC = 4
NXC = 64
N_GY = 4
N_GX = 2


def place_ends(entries, rng, smallest, top_value):
    shape = entries.shape
    spot = [jax.random.randint(jax.random.fold_in(rng, axis), (), 0, shape[axis]) for axis in range(len(shape))]
    entries = entries.at[tuple(spot)].set(smallest)
    longest = shape.index(max(shape))
    spot[longest] = (spot[longest] + 1) % shape[longest]
    return entries.at[tuple(spot)].set(top_value)


def shard_levels(own_key, dims, pieces, least, high):
    factor_of = 1.0
    for dim, parts in pieces:
        heights = jax.random.uniform(jax.random.fold_in(jax.random.fold_in(own_key, 6), dim), (parts,), jnp.float32, least / len(pieces), high / len(pieces))
        factor_of = factor_of * jnp.repeat(jnp.exp(heights), dims[dim] // parts).reshape((-1,) + (1,) * (len(dims) - 1 - dim))
    return factor_of


def noise(key, dims, width, most, pieces=(), held_as=jnp.bfloat16):
    loudness = shard_levels(key, dims, pieces, -0.22, 0.18) if pieces else 1.0
    array = jax.random.normal(key, dims, jnp.float32) * width * loudness
    return jnp.minimum(jnp.maximum(array, -most), most).astype(held_as)


def setup_inputs(seed: int = 0, part: int = 0) -> dict:
    seeds = jax.random.split(jax.random.key(seed), 11)
    own_keys = jax.random.split(jax.random.fold_in(seeds[10], part), 11)
    fine_in = noise(own_keys[0], (CF, FZ, NYF, NXF), 1.0, 6.0, ((0, 2), (2, 4), (3, 2)), jnp.float32)
    context_in = noise(own_keys[1], (CC, BZ, NYC, NXC), 1.0, 6.0, ((0, 2), (2, 4), (3, 2)), jnp.float32)
    weight_fine = noise(seeds[2], (3, 3, 3, CF, CF), (27 * CF) ** -0.5, 0.21875, ((4, 2),), jnp.float32)
    weight_coarse = noise(seeds[3], (3, 3, 3, CC, CC), (27 * CC) ** -0.5, 0.15625, ((4, 2),), jnp.float32)
    lift_weight = noise(seeds[4], (CC, CF), CC ** -0.5, 0.75, ((1, 2),), jnp.float32)
    lower_weight = noise(seeds[5], (CF, CC), CF ** -0.5, 1.0, ((1, 2),), jnp.float32)
    block_row = place_ends(jax.random.randint(own_keys[6], (TY, TX), 0, TY), jax.random.fold_in(own_keys[6], 1), 0, TY - 1).astype(jnp.int32)
    tile_count = place_ends(jax.random.randint(own_keys[7], (TY, TX), 1, 5), jax.random.fold_in(own_keys[7], 1), 1, 4).astype(jnp.int32)
    fine_cotangent = noise(own_keys[8], (CF, FZ, NYF, NXF), 1.0, 6.0, ((0, 2), (2, 4), (3, 2)), jnp.float32)
    coarse_cotangent = noise(own_keys[9], (CC, BZ, NYC, NXC), 1.0, 6.0, ((0, 2), (2, 4), (3, 2)), jnp.float32)
    return {"fine_in": fine_in, "context_in": context_in, "weight_fine": weight_fine, "weight_coarse": weight_coarse, "lift_weight": lift_weight, "lower_weight": lower_weight, "block_row": block_row, "tile_count": tile_count, "fine_cotangent": fine_cotangent, "coarse_cotangent": coarse_cotangent}


precise = lax.Precision.HIGHEST

def convolve(volume, kernel):
    output = lax.conv_general_dilated(volume[None], kernel, (1, 1, 1), 'SAME', dimension_numbers=('NCDHW', 'DHWIO', 'NCDHW'), precision=precise)
    return output[0]

def refine(block):
    return jnp.repeat(jnp.repeat(jnp.repeat(block, RATIO, 1), RATIO, 2), RATIO, 3)

def joining_pass(fine_in, context_in, weight_fine, weight_coarse, lift_weight, lower_weight, selector, counts):
    fine_hidden = jax.nn.silu(convolve(fine_in, weight_fine))
    coarse_hidden = jax.nn.silu(convolve(context_in, weight_coarse))
    lifted = jnp.einsum('czyx,cf->fzyx', coarse_hidden, lift_weight, precision=precise)
    blocks = lifted.reshape(CF, BZ, N_GY, BY, N_GX, BX)
    chosen = jnp.einsum('jik,fzkyix->fzjyix', selector, blocks, precision=precise)
    chosen = chosen.reshape(CF, BZ, NYC, NXC)
    joined_fine = fine_hidden + refine(chosen)
    tile_means = fine_hidden.reshape(CF, BZ, RATIO, NYC, RATIO, NXC, RATIO).mean(axis=(2, 4, 6))
    tile_blocks = tile_means.reshape(CF, BZ, N_GY, BY, N_GX, BX)
    weighted = selector * counts[:, :, None]
    summed = jnp.einsum('jik,fzjyix->fzkyix', weighted, tile_blocks, precision=precise)
    divisor = jnp.maximum(lax.optimization_barrier(jnp.sum(weighted, axis=0)), 1.0)
    averaged = summed / divisor.T[None, None, :, None, :, None]
    averaged = averaged.reshape(CF, BZ, NYC, NXC)
    lowered = jnp.einsum('fzyx,fc->czyx', averaged, lower_weight, precision=precise)
    return (joined_fine, coarse_hidden + lowered)

def reference(fine_in, context_in, weight_fine, weight_coarse, lift_weight, lower_weight, block_row, tile_count, fine_cotangent, coarse_cotangent):
    positions = jnp.arange(N_GY, dtype=jnp.int32)
    selector = (block_row[:, :, None] == positions[None, None, :]).astype(jnp.float32)
    counts = tile_count.astype(jnp.float32)

    def forward(kernel_fine, kernel_coarse, lift_matrix, lower_matrix):
        return joining_pass(fine_in, context_in, kernel_fine, kernel_coarse, lift_matrix, lower_matrix, selector, counts)
    outputs, pullback = jax.vjp(forward, weight_fine, weight_coarse, lift_weight, lower_weight)
    fine_scale = (FZ * NYF * NXF) ** (-0.5)
    coarse_scale = (BZ * NYC * NXC) ** (-0.5)
    gradients = pullback((fine_cotangent * fine_scale, coarse_cotangent * coarse_scale))
    return (outputs[0], outputs[1], gradients[0], gradients[1], gradients[2], gradients[3])
```

```python
import functools

import jax
import jax.numpy as jnp
from jax import lax
from jax.experimental import pallas as pl
from jax.experimental.pallas import tpu as pltpu
from jax.sharding import PartitionSpec as P

RATIO = 4


precise = lax.Precision.HIGH


def pad_depth(volume):
    return jnp.pad(volume, ((0, 0), (1, 1), (0, 0), (0, 0)))


def shifted_stack(padded, shift_z, shift_y, extent_z, extent_y, extent_x):
    return jnp.stack(
        [
            padded[
                :,
                shift_z : shift_z + extent_z,
                shift_y : shift_y + extent_y,
                shift_x : shift_x + extent_x,
            ]
            for shift_x in range(3)
        ]
    )


def convolve(padded, kernel):
    extent_z = padded.shape[1] - 2
    extent_y = padded.shape[2] - 2
    extent_x = padded.shape[3] - 2
    result = jnp.zeros((kernel.shape[4], extent_z, extent_y, extent_x), jnp.float32)
    for shift_z in range(3):
        for shift_y in range(3):
            stacked = shifted_stack(padded, shift_z, shift_y, extent_z, extent_y, extent_x)
            result = result + jnp.einsum(
                "aizyx,aio->ozyx", stacked, kernel[shift_z, shift_y], precision=precise
            )
    return result


def kernel_terms(padded, seed):
    extent_z = seed.shape[1]
    extent_y = seed.shape[2]
    extent_x = seed.shape[3]
    layers_z = []
    for shift_z in range(3):
        layers_y = []
        for shift_y in range(3):
            stacked = shifted_stack(padded, shift_z, shift_y, extent_z, extent_y, extent_x)
            layers_y.append(jnp.einsum("aizyx,ozyx->aio", stacked, seed, precision=precise))
        layers_z.append(jnp.stack(layers_y))
    return jnp.stack(layers_z)


def silu_slope(value):
    logistic = jax.nn.sigmoid(value)
    return logistic * (1.0 + value * (1.0 - logistic))


def refine(block):
    channels, extent_z, extent_y, extent_x = block.shape
    grown = jnp.broadcast_to(
        block[:, :, None, :, None, :, None],
        (channels, extent_z, RATIO, extent_y, RATIO, extent_x, RATIO),
    )
    return grown.reshape(channels, extent_z * RATIO, extent_y * RATIO, extent_x * RATIO)


def group_view(volume):
    channels, extent_z, extent_y, extent_x = volume.shape
    return volume.reshape(
        channels, extent_z // RATIO, RATIO, extent_y // RATIO, RATIO, extent_x // RATIO, RATIO
    )


LANES = 128
AXES = ("gy", "gx", "col")
MESH = pl.DeviceIdType.MESH
IN_VMEM = pl.BlockSpec(memory_space=pltpu.VMEM)


def near_keys(rows, columns):
    return sorted({(a % rows, b % columns) for a in (-1, 0, 1) for b in (-1, 0, 1)})


def peer(sizes, offset):
    return {
        axis: lax.rem(lax.axis_index(axis) + step, size) if step else lax.axis_index(axis)
        for axis, size, step in zip(AXES, sizes, offset)
    }


def greet(sizes, offsets):
    barrier = pltpu.get_barrier_semaphore()
    for offset in offsets:
        pl.semaphore_signal(barrier, inc=1, device_id=peer(sizes, offset), device_id_type=MESH)
    pl.semaphore_wait(barrier, len(offsets))


def opening_plan(sizes):
    rows, columns, cores = sizes
    plan = []
    for core in range(1, cores):
        plan.append(("whole", (0, 0, core)))
    for core in range(cores):
        plan.append(("last", (1, 0, core)))
        plan.append(("first", (rows - 1, 0, core)))
    for a, b in near_keys(rows, columns):
        for core in range(cores):
            if (a, b, core) != (0, 0, 0):
                plan.append(("near", (a, b, core)))
    for a in range(rows):
        for core in range(cores):
            if (a, core) != (0, 0):
                plan.append(("line", (a, 0, core)))
    return plan


def both_ways(sizes, plan):
    found = {offset for _, offset in plan}
    found |= {tuple((n - s) % n for n, s in zip(sizes, offset)) for offset in found}
    return sorted(found)


def opening_kernel(sizes, fine, near, line, whole_out, face_out, near_out, line_out, send, recv):
    rows, columns, _ = sizes
    plan = opening_plan(sizes)
    keys = near_keys(rows, columns)
    row_here, core_here = lax.axis_index("gy"), lax.axis_index("col")
    greet(sizes, both_ways(sizes, plan))
    height = fine.shape[1]
    copies = []
    for index, (kind, offset) in enumerate(plan):
        if kind == "whole":
            ends = (fine, whole_out.at[core_here])
        elif kind == "last":
            ends = (fine.at[:, height - 1], face_out.at[0, core_here])
        elif kind == "first":
            ends = (fine.at[:, 0], face_out.at[1, core_here])
        elif kind == "near":
            slot = keys.index(((rows - offset[0]) % rows, (columns - offset[1]) % columns))
            ends = (near, near_out.at[slot, core_here])
        else:
            ends = (line, line_out.at[row_here, core_here])
        copy = pltpu.make_async_remote_copy(
            src_ref=ends[0],
            dst_ref=ends[1],
            send_sem=send.at[index],
            recv_sem=recv.at[index],
            device_id=peer(sizes, offset),
            device_id_type=MESH,
        )
        copy.start()
        copies.append(copy)
    whole_out[core_here] = fine[...]
    near_out[keys.index((0, 0)), core_here] = near[...]
    line_out[row_here, core_here] = line[...]
    for copy in copies:
        copy.wait()


def opening(sizes, fine, near, line):
    rows, columns, cores = sizes
    number = len(opening_plan(sizes))
    depth, _, channels, wide = fine.shape
    return pl.pallas_call(
        functools.partial(opening_kernel, sizes),
        out_shape=(
            jax.ShapeDtypeStruct((cores, *fine.shape), jnp.float32),
            jax.ShapeDtypeStruct((2, cores, depth, channels, wide), jnp.float32),
            jax.ShapeDtypeStruct((len(near_keys(rows, columns)), cores, *near.shape), jnp.float32),
            jax.ShapeDtypeStruct((rows, cores, *line.shape), jnp.float32),
        ),
        in_specs=[IN_VMEM] * 3,
        out_specs=[IN_VMEM] * 4,
        scratch_shapes=[pltpu.SemaphoreType.DMA((number,)), pltpu.SemaphoreType.DMA((number,))],
        compiler_params=pltpu.CompilerParams(
            collective_id=0, has_side_effects=True, vmem_limit_bytes=48 << 20
        ),
    )(fine, near, line)


def line_kernel(sizes, line, line_out, send, recv):
    rows, _, cores = sizes
    offsets = [(a, 0, c) for a in range(rows) for c in range(cores) if (a, c) != (0, 0)]
    row_here, core_here = lax.axis_index("gy"), lax.axis_index("col")
    greet(sizes, offsets)
    copies = []
    for index, offset in enumerate(offsets):
        copy = pltpu.make_async_remote_copy(
            src_ref=line,
            dst_ref=line_out.at[row_here, core_here],
            send_sem=send.at[index],
            recv_sem=recv.at[index],
            device_id=peer(sizes, offset),
            device_id_type=MESH,
        )
        copy.start()
        copies.append(copy)
    line_out[row_here, core_here] = line[...]
    for copy in copies:
        copy.wait()


def line_gather(sizes, line):
    rows, _, cores = sizes
    number = rows * cores - 1
    return pl.pallas_call(
        functools.partial(line_kernel, sizes),
        out_shape=jax.ShapeDtypeStruct((rows, cores, *line.shape), jnp.float32),
        in_specs=[IN_VMEM],
        out_specs=IN_VMEM,
        scratch_shapes=[pltpu.SemaphoreType.DMA((number,)), pltpu.SemaphoreType.DMA((number,))],
        compiler_params=pltpu.CompilerParams(collective_id=1, has_side_effects=True),
    )(line)


def total_kernel(sizes, parts, result, landed, send, recv, send_back, recv_back):
    rows, columns, _ = sizes
    offsets = [(a, b, 0) for a in range(rows) for b in range(columns) if (a, b) != (0, 0)]

    def place(offset):
        target = peer(sizes, offset)
        return target["gy"] * columns + target["gx"]

    here = lax.axis_index("gy") * columns + lax.axis_index("gx")
    greet(sizes, offsets)
    copies = []
    for index, offset in enumerate(offsets):
        copy = pltpu.make_async_remote_copy(
            src_ref=parts.at[place(offset)],
            dst_ref=landed.at[index],
            send_sem=send.at[index],
            recv_sem=recv.at[index],
            device_id=peer(sizes, offset),
            device_id_type=MESH,
        )
        copy.start()
        copies.append(copy)
    total = parts[here]
    for index, copy in enumerate(copies):
        copy.wait()
        total = total + landed[index]
    result[here] = total
    copies = []
    for index, offset in enumerate(offsets):
        copy = pltpu.make_async_remote_copy(
            src_ref=result.at[here],
            dst_ref=result.at[here],
            send_sem=send_back.at[index],
            recv_sem=recv_back.at[index],
            device_id=peer(sizes, offset),
            device_id_type=MESH,
        )
        copy.start()
        copies.append(copy)
    for copy in copies:
        copy.wait()


def total_over_tiles(sizes, arrays):
    rows, columns, _ = sizes
    peers = rows * columns
    flat = jnp.concatenate([array.reshape(-1, LANES) for array in arrays])
    chunk = -(-flat.shape[0] // (8 * peers)) * 8
    parts = jnp.pad(flat, ((0, peers * chunk - flat.shape[0]), (0, 0))).reshape(peers, chunk, LANES)
    number = peers - 1
    result = pl.pallas_call(
        functools.partial(total_kernel, sizes),
        out_shape=jax.ShapeDtypeStruct(parts.shape, jnp.float32),
        in_specs=[IN_VMEM],
        out_specs=IN_VMEM,
        scratch_shapes=[pltpu.VMEM((number, chunk, LANES), jnp.float32)]
        + [pltpu.SemaphoreType.DMA((number,))] * 4,
        compiler_params=pltpu.CompilerParams(collective_id=2, has_side_effects=True),
    )(parts)
    result = result.reshape(peers * chunk, LANES)
    given, start = [], 0
    for array in arrays:
        count = array.size // LANES
        given.append(result[start : start + count].reshape(array.shape))
        start += count
    return tuple(given)


def as_rows(*arrays):
    return jnp.concatenate([array.reshape(-1, LANES) for array in arrays])


def local(
    sizes,
    fine_in,
    context_in,
    weight_fine,
    weight_coarse,
    lift_weight,
    lower_weight,
    block_row,
    tile_count,
    fine_cotangent,
    coarse_cotangent,
):
    rows_total, columns_total, cores = sizes
    column_here, row_here, core_here = (lax.axis_index(a) for a in ("gx", "gy", "col"))
    column_rows = lax.dynamic_slice_in_dim(block_row, column_here, 1, 1)[:, 0]
    column_counts = lax.dynamic_slice_in_dim(tile_count, column_here, 1, 1)[:, 0].astype(
        jnp.float32
    )
    target = lax.dynamic_slice_in_dim(column_rows, row_here, 1, 0)[0]
    own_count = lax.dynamic_slice_in_dim(column_counts, row_here, 1, 0)[0]
    routed_here = (column_rows == row_here).astype(jnp.float32)
    weights_here = routed_here * column_counts
    divisor_here = jnp.maximum(jnp.sum(weights_here), 1.0)
    divisor_target = jnp.maximum(
        jnp.sum(jnp.where(column_rows == target, column_counts, 0.0)), 1.0
    )
    channels, depth, height, wide = fine_in.shape
    broad, low, short, narrow = context_in.shape
    fine_cells = depth * height * rows_total * wide * columns_total
    coarse_cells = low * short * rows_total * narrow * columns_total
    fine_seed = fine_cotangent * fine_cells ** (-0.5)
    coarse_seed_own = coarse_cotangent * coarse_cells ** (-0.5)
    group_seed = jnp.sum(group_view(fine_seed), axis=(2, 4, 6))

    fine_rows = fine_in.transpose(1, 2, 0, 3)
    edges = jnp.stack([fine_in[..., 0], fine_in[..., wide - 1]])
    near = as_rows(context_in, edges)
    line = as_rows(coarse_seed_own, group_seed, lift_weight, lower_weight)
    whole, faces, nears, lines = opening(sizes, fine_rows, near, line)

    keys = near_keys(rows_total, columns_total)
    context_rows = context_in.size // LANES
    contexts = nears[:, :, :context_rows].reshape(
        len(keys), cores * broad, low, short, narrow
    )
    sides = nears[:, :, context_rows:].reshape(len(keys), cores, 2, channels, depth, height)

    def inside(a, b):
        row, column = row_here + a, column_here + b
        return (row >= 0) & (row < rows_total) & (column >= 0) & (column < columns_total)

    def key(a, b):
        return keys.index((a % rows_total, b % columns_total))

    def kept(a, b, value):
        return value if a == 0 and b == 0 else jnp.where(inside(a, b), value, 0.0)

    def context_piece(a, b):
        block = contexts[key(a, b)]
        block = block[:, :, -1:] if a < 0 else block[:, :, :1] if a > 0 else block
        block = block[..., -1:] if b < 0 else block[..., :1] if b > 0 else block
        return kept(a, b, block)

    coarse_pad = pad_depth(
        jnp.concatenate(
            [
                jnp.concatenate([context_piece(a, b) for b in (-1, 0, 1)], axis=3)
                for a in (-1, 0, 1)
            ],
            axis=2,
        )
    )

    def edge_piece(a, b):
        edge = sides[key(a, b), :, 1 if b < 0 else 0].reshape(cores * channels, depth, height)
        edge = edge[:, :, -1:] if a < 0 else edge[:, :, :1] if a > 0 else edge
        return kept(a, b, edge)[..., None]

    def edge_column(b):
        return jnp.concatenate([edge_piece(a, b) for a in (-1, 0, 1)], axis=2)

    def face(a):
        rows = faces[0 if a < 0 else 1].transpose(0, 2, 1, 3).reshape(cores * channels, depth, wide)
        return kept(a, 0, rows)[:, :, None]

    fine_all = whole.transpose(0, 3, 1, 2, 4).reshape(cores * channels, depth, height, wide)
    fine_pad = pad_depth(
        jnp.concatenate(
            [
                edge_column(-1),
                jnp.concatenate([face(-1), fine_all, face(1)], axis=2),
                edge_column(1),
            ],
            axis=3,
        )
    )

    first = coarse_cotangent.size // LANES
    second = first + group_seed.size // LANES
    third = second + lift_weight.size // LANES
    seeds = lines[:, :, :first].reshape(rows_total, cores * broad, low, short, narrow)
    groups = lines[:, :, first:second].reshape(
        rows_total, cores * channels, low, short, narrow
    )
    weights_all = lax.dynamic_index_in_dim(lines, row_here, 0, False)
    lift_all = weights_all[:, second:third].reshape(cores, *lift_weight.shape)
    lower_all = weights_all[:, third:].reshape(cores, *lower_weight.shape)

    lifted_seed_all = jnp.einsum("r,rfzyx->fzyx", routed_here, groups, precision=lax.Precision.HIGHEST)
    lifted_seed = lax.dynamic_slice_in_dim(lifted_seed_all, core_here * channels, channels, 0)
    lift_own = lax.dynamic_slice_in_dim(lift_all, core_here * broad, broad, 1)
    coarse_total_seed = coarse_seed_own + jnp.einsum(
        "kcf,kfzyx->czyx",
        lift_own,
        lifted_seed_all.reshape(cores, channels, low, short, narrow),
        precision=precise,
    )
    lower_own = lax.dynamic_slice_in_dim(lower_all, core_here * channels, channels, 1)
    target_seed = lax.dynamic_index_in_dim(seeds, target, 0, False)
    tile_seed = jnp.einsum(
        "kfc,kczyx->fzyx",
        lower_own,
        target_seed.reshape(cores, broad, low, short, narrow),
        precision=precise,
    ) * (own_count / (RATIO * RATIO * RATIO) / divisor_target)

    coarse_pre = convolve(coarse_pad, weight_coarse)
    coarse_hidden = jax.nn.silu(coarse_pre)
    fine_pre = convolve(fine_pad, weight_fine)
    fine_hidden = jax.nn.silu(fine_pre)
    tile_means = group_view(fine_hidden).mean(axis=(2, 4, 6))
    middle = line_gather(sizes, as_rows(coarse_hidden, tile_means))
    hiddens = middle[:, :, :first].reshape(rows_total, cores * broad, low, short, narrow)
    means = middle[:, :, first:].reshape(rows_total, cores * channels, low, short, narrow)
    coarse_wide = lax.dynamic_index_in_dim(hiddens, row_here, 0, False)
    chosen = jnp.einsum(
        "czyx,cf->fzyx",
        lax.dynamic_index_in_dim(hiddens, target, 0, False),
        lift_weight,
        precision=precise,
    )
    joined_fine = fine_hidden + refine(chosen)
    averaged_wide = (
        jnp.einsum("r,rfzyx->fzyx", weights_here, means, precision=lax.Precision.HIGHEST) / divisor_here
    )
    joined_coarse = coarse_hidden + jnp.einsum(
        "fzyx,fc->czyx", averaged_wide, lower_weight, precision=precise
    )
    lower_gradient = jnp.einsum("fzyx,czyx->fc", averaged_wide, coarse_seed_own, precision=precise)
    lift_gradient = jnp.einsum("czyx,fzyx->cf", coarse_wide, lifted_seed, precision=precise)
    hidden_seed = fine_seed + refine(tile_seed)
    coarse_gradient = kernel_terms(coarse_pad, coarse_total_seed * silu_slope(coarse_pre))
    fine_gradient = kernel_terms(fine_pad, hidden_seed * silu_slope(fine_pre))
    fine_gradient, coarse_gradient, lift_gradient, lower_gradient = total_over_tiles(
        sizes, (fine_gradient, coarse_gradient, lift_gradient, lower_gradient)
    )
    return (
        joined_fine,
        joined_coarse,
        fine_gradient,
        coarse_gradient,
        lift_gradient,
        lower_gradient,
    )


def solution(mesh):
    sizes = tuple(mesh.shape[axis] for axis in AXES)
    in_specs = (
        P("col", "grp", "gy", "gx"),
        P("col", "grp", "gy", "gx"),
        P(None, None, None, None, "col"),
        P(None, None, None, None, "col"),
        P(None, "col"),
        P(None, "col"),
        P("grp", None),
        P("grp", None),
        P("col", "grp", "gy", "gx"),
        P("col", "grp", "gy", "gx"),
    )
    out_specs = (
        P("col", "grp", "gy", "gx"),
        P("col", "grp", "gy", "gx"),
        P("grp", None, None, None, "col"),
        P("grp", None, None, None, "col"),
        P("grp", "col"),
        P("grp", "col"),
    )
    return jax.shard_map(
        functools.partial(local, sizes),
        mesh=mesh,
        in_specs=in_specs,
        out_specs=out_specs,
        check_vma=False,
    )
```

```python
import functools

import jax
import jax.numpy as jnp
from jax import lax
from jax.experimental import pallas as pl
from jax.experimental.pallas import tpu as pltpu
from jax.sharding import PartitionSpec as P

RATIO = 4


precise = lax.Precision.HIGH


def pad_depth(volume):
    return jnp.pad(volume, ((0, 0), (1, 1), (0, 0), (0, 0)))


def shifted_stack(padded, shift_z, shift_y, extent_z, extent_y, extent_x):
    return jnp.stack(
        [
            padded[
                :,
                shift_z : shift_z + extent_z,
                shift_y : shift_y + extent_y,
                shift_x : shift_x + extent_x,
            ]
            for shift_x in range(3)
        ]
    )


def convolve(padded, kernel):
    extent_z = padded.shape[1] - 2
    extent_y = padded.shape[2] - 2
    extent_x = padded.shape[3] - 2
    result = jnp.zeros((kernel.shape[4], extent_z, extent_y, extent_x), jnp.float32)
    for shift_z in range(3):
        for shift_y in range(3):
            stacked = shifted_stack(padded, shift_z, shift_y, extent_z, extent_y, extent_x)
            result = result + jnp.einsum(
                "aizyx,aio->ozyx", stacked, kernel[shift_z, shift_y], precision=precise
            )
    return result


def kernel_terms(padded, seed):
    extent_z = seed.shape[1]
    extent_y = seed.shape[2]
    extent_x = seed.shape[3]
    layers_z = []
    for shift_z in range(3):
        layers_y = []
        for shift_y in range(3):
            stacked = shifted_stack(padded, shift_z, shift_y, extent_z, extent_y, extent_x)
            layers_y.append(jnp.einsum("aizyx,ozyx->aio", stacked, seed, precision=precise))
        layers_z.append(jnp.stack(layers_y))
    return jnp.stack(layers_z)


def silu_slope(value):
    logistic = jax.nn.sigmoid(value)
    return logistic * (1.0 + value * (1.0 - logistic))


def refine(block):
    channels, extent_z, extent_y, extent_x = block.shape
    grown = jnp.broadcast_to(
        block[:, :, None, :, None, :, None],
        (channels, extent_z, RATIO, extent_y, RATIO, extent_x, RATIO),
    )
    return grown.reshape(channels, extent_z * RATIO, extent_y * RATIO, extent_x * RATIO)


def group_view(volume):
    channels, extent_z, extent_y, extent_x = volume.shape
    return volume.reshape(
        channels, extent_z // RATIO, RATIO, extent_y // RATIO, RATIO, extent_x // RATIO, RATIO
    )


LANES = 128
AXES = ("gy", "gx", "col")
MESH = pl.DeviceIdType.MESH
IN_VMEM = pl.BlockSpec(memory_space=pltpu.VMEM)


def near_keys(rows, columns):
    return sorted({(a % rows, b % columns) for a in (-1, 0, 1) for b in (-1, 0, 1)})


def peer(sizes, offset):
    return {
        axis: lax.rem(lax.axis_index(axis) + step, size) if step else lax.axis_index(axis)
        for axis, size, step in zip(AXES, sizes, offset)
    }


def greet(sizes, offsets):
    barrier = pltpu.get_barrier_semaphore()
    for offset in offsets:
        pl.semaphore_signal(barrier, inc=1, device_id=peer(sizes, offset), device_id_type=MESH)
    pl.semaphore_wait(barrier, len(offsets))


def opening_plan(sizes):
    rows, columns, cores = sizes
    plan = []
    for core in range(1, cores):
        plan.append(("whole", (0, 0, core)))
    for core in range(cores):
        plan.append(("last", (1, 0, core)))
        plan.append(("first", (rows - 1, 0, core)))
    for a, b in near_keys(rows, columns):
        for core in range(cores):
            if (a, b, core) != (0, 0, 0):
                plan.append(("near", (a, b, core)))
    for a in range(rows):
        for core in range(cores):
            if (a, core) != (0, 0):
                plan.append(("line", (a, 0, core)))
    return plan


def both_ways(sizes, plan):
    found = {offset for _, offset in plan}
    found |= {tuple((n - s) % n for n, s in zip(sizes, offset)) for offset in found}
    return sorted(found)


def opening_kernel(sizes, fine, near, line, whole_out, face_out, near_out, line_out, send, recv):
    rows, columns, _ = sizes
    plan = opening_plan(sizes)
    keys = near_keys(rows, columns)
    row_here, core_here = lax.axis_index("gy"), lax.axis_index("col")
    greet(sizes, both_ways(sizes, plan))
    height = fine.shape[1]
    copies = []
    for index, (kind, offset) in enumerate(plan):
        if kind == "whole":
            ends = (fine, whole_out.at[core_here])
        elif kind == "last":
            ends = (fine.at[:, height - 1], face_out.at[0, core_here])
        elif kind == "first":
            ends = (fine.at[:, 0], face_out.at[1, core_here])
        elif kind == "near":
            slot = keys.index(((rows - offset[0]) % rows, (columns - offset[1]) % columns))
            ends = (near, near_out.at[slot, core_here])
        else:
            ends = (line, line_out.at[row_here, core_here])
        copy = pltpu.make_async_remote_copy(
            src_ref=ends[0],
            dst_ref=ends[1],
            send_sem=send.at[index],
            recv_sem=recv.at[index],
            device_id=peer(sizes, offset),
            device_id_type=MESH,
        )
        copy.start()
        copies.append(copy)
    whole_out[core_here] = fine[...]
    near_out[keys.index((0, 0)), core_here] = near[...]
    line_out[row_here, core_here] = line[...]
    for copy in copies:
        copy.wait()


def opening(sizes, fine, near, line):
    rows, columns, cores = sizes
    number = len(opening_plan(sizes))
    depth, _, channels, wide = fine.shape
    return pl.pallas_call(
        functools.partial(opening_kernel, sizes),
        out_shape=(
            jax.ShapeDtypeStruct((cores, *fine.shape), jnp.float32),
            jax.ShapeDtypeStruct((2, cores, depth, channels, wide), jnp.float32),
            jax.ShapeDtypeStruct((len(near_keys(rows, columns)), cores, *near.shape), jnp.float32),
            jax.ShapeDtypeStruct((rows, cores, *line.shape), jnp.float32),
        ),
        in_specs=[IN_VMEM] * 3,
        out_specs=[IN_VMEM] * 4,
        scratch_shapes=[pltpu.SemaphoreType.DMA((number,)), pltpu.SemaphoreType.DMA((number,))],
        compiler_params=pltpu.CompilerParams(
            collective_id=0, has_side_effects=True, vmem_limit_bytes=48 << 20
        ),
    )(fine, near, line)


def line_kernel(sizes, line, line_out, send, recv):
    rows, _, cores = sizes
    offsets = [(a, 0, c) for a in range(rows) for c in range(cores) if (a, c) != (0, 0)]
    row_here, core_here = lax.axis_index("gy"), lax.axis_index("col")
    greet(sizes, offsets)
    copies = []
    for index, offset in enumerate(offsets):
        copy = pltpu.make_async_remote_copy(
            src_ref=line,
            dst_ref=line_out.at[row_here, core_here],
            send_sem=send.at[index],
            recv_sem=recv.at[index],
            device_id=peer(sizes, offset),
            device_id_type=MESH,
        )
        copy.start()
        copies.append(copy)
    line_out[row_here, core_here] = line[...]
    for copy in copies:
        copy.wait()


def line_gather(sizes, line):
    rows, _, cores = sizes
    number = rows * cores - 1
    return pl.pallas_call(
        functools.partial(line_kernel, sizes),
        out_shape=jax.ShapeDtypeStruct((rows, cores, *line.shape), jnp.float32),
        in_specs=[IN_VMEM],
        out_specs=IN_VMEM,
        scratch_shapes=[pltpu.SemaphoreType.DMA((number,)), pltpu.SemaphoreType.DMA((number,))],
        compiler_params=pltpu.CompilerParams(collective_id=1, has_side_effects=True),
    )(line)


def total_kernel(sizes, parts, result, landed, send, recv, send_back, recv_back):
    rows, columns, _ = sizes
    offsets = [(a, b, 0) for a in range(rows) for b in range(columns) if (a, b) != (0, 0)]

    def place(offset):
        target = peer(sizes, offset)
        return target["gy"] * columns + target["gx"]

    here = lax.axis_index("gy") * columns + lax.axis_index("gx")
    greet(sizes, offsets)
    copies = []
    for index, offset in enumerate(offsets):
        copy = pltpu.make_async_remote_copy(
            src_ref=parts.at[place(offset)],
            dst_ref=landed.at[index],
            send_sem=send.at[index],
            recv_sem=recv.at[index],
            device_id=peer(sizes, offset),
            device_id_type=MESH,
        )
        copy.start()
        copies.append(copy)
    total = parts[here]
    for index, copy in enumerate(copies):
        copy.wait()
        total = total + landed[index]
    result[here] = total
    copies = []
    for index, offset in enumerate(offsets):
        copy = pltpu.make_async_remote_copy(
            src_ref=result.at[here],
            dst_ref=result.at[here],
            send_sem=send_back.at[index],
            recv_sem=recv_back.at[index],
            device_id=peer(sizes, offset),
            device_id_type=MESH,
        )
        copy.start()
        copies.append(copy)
    for copy in copies:
        copy.wait()


def total_over_tiles(sizes, arrays):
    rows, columns, _ = sizes
    peers = rows * columns
    flat = jnp.concatenate([array.reshape(-1, LANES) for array in arrays])
    chunk = -(-flat.shape[0] // (8 * peers)) * 8
    parts = jnp.pad(flat, ((0, peers * chunk - flat.shape[0]), (0, 0))).reshape(peers, chunk, LANES)
    number = peers - 1
    result = pl.pallas_call(
        functools.partial(total_kernel, sizes),
        out_shape=jax.ShapeDtypeStruct(parts.shape, jnp.float32),
        in_specs=[IN_VMEM],
        out_specs=IN_VMEM,
        scratch_shapes=[pltpu.VMEM((number, chunk, LANES), jnp.float32)]
        + [pltpu.SemaphoreType.DMA((number,))] * 4,
        compiler_params=pltpu.CompilerParams(collective_id=2, has_side_effects=True),
    )(parts)
    result = result.reshape(peers * chunk, LANES)
    given, start = [], 0
    for array in arrays:
        count = array.size // LANES
        given.append(result[start : start + count].reshape(array.shape))
        start += count
    return tuple(given)


def halves(value):
    high = value.astype(jnp.bfloat16)
    return high, (value - high.astype(jnp.float32)).astype(jnp.bfloat16)


def fine_kernel(whole, faces, edges, weight, seed, hidden, means, gradient, taps, slopes, sums):
    cores, depth, height, channels, wide = whole.shape
    inputs = cores * channels
    outputs = seed.shape[1]
    span = height * wide
    lanes = lax.broadcasted_iota(jnp.int32, (inputs, wide), 1)
    weight_all = jnp.concatenate(halves(weight[...]), axis=0)
    half = weight_all.shape[0] // 2
    for z in (0, depth + 1):
        slopes[z] = jnp.zeros(slopes.shape[1:], slopes.dtype)
    pooled = []

    def finish(z):
        value = sums[z]
        logistic = jax.nn.sigmoid(value)
        active = value * logistic
        hidden[z] = active
        high, rest = halves(seed[z] * (logistic * (1.0 + value * (1.0 - logistic))))
        slopes[z + 1, :outputs] = high
        slopes[z + 1, outputs:] = rest
        rows = sum(active[:, y * wide : (y + 1) * wide] for y in range(height))
        if z % RATIO == 0:
            pooled.append(rows)
        else:
            pooled[-1] = pooled[-1] + rows

    for z in range(depth):
        for y in range(height + 2):
            if y == 0:
                row = faces[0, :, z]
            elif y == height + 1:
                row = faces[1, :, z]
            else:
                row = whole[:, z, y - 1]
            row = row.reshape(inputs, wide)
            left = jnp.where(lanes == 0, edges[0, z][:, y : y + 1], pltpu.roll(row, 1, 1))
            right = jnp.where(
                lanes == wide - 1, edges[1, z][:, y : y + 1], pltpu.roll(row, wide - 1, 1)
            )
            high, rest = halves(jnp.concatenate([left, row, right], axis=0))
            place = slice(y * wide, (y + 1) * wide)
            taps[z, : 3 * inputs, place] = high
            taps[z, 3 * inputs :, place] = rest
        product = jnp.dot(weight_all, taps[z], preferred_element_type=jnp.float32)
        for dz in range(3):
            goal = z - dz + 1
            if not 0 <= goal < depth:
                continue
            term = None
            for dy in range(3):
                at = (dz * 3 + dy) * outputs
                for start in (at, half + at):
                    piece = product[start : start + outputs, dy * wide : dy * wide + span]
                    term = piece if term is None else term + piece
            sums[goal] = term if z == max(goal - 1, 0) else sums[goal] + term
        if z:
            finish(z - 1)
    finish(depth - 1)
    groups = wide // RATIO
    pool = (
        lax.broadcasted_iota(jnp.int32, (wide, groups), 0) // RATIO
        == lax.broadcasted_iota(jnp.int32, (wide, groups), 1)
    ).astype(jnp.float32)
    for index, rows in enumerate(pooled):
        means[index] = jnp.dot(
            rows, pool, precision=lax.Precision.HIGHEST, preferred_element_type=jnp.float32
        ) * (1.0 / RATIO**3)
    for dy in range(3):
        total = None
        for z in range(depth):
            term = lax.dot_general(
                slopes[z : z + 3].reshape(6 * outputs, span),
                taps[z, :, dy * wide : dy * wide + span],
                (((1,), (1,)), ((), ())),
                preferred_element_type=jnp.float32,
            )
            total = term if total is None else total + term
        for place in range(3):
            at = place * 2 * outputs
            gradient[2 - place, dy] = (
                total[at : at + outputs] + total[at + outputs : at + 2 * outputs]
            )


def fine_pass(whole, faces, edges, weight_fine, seed):
    cores, depth, height, channels, wide = whole.shape
    inputs, outputs = weight_fine.shape[3:]
    weight = weight_fine.transpose(0, 1, 4, 2, 3).reshape(9 * outputs, 3 * inputs)
    hidden, means, gradient = pl.pallas_call(
        fine_kernel,
        out_shape=(
            jax.ShapeDtypeStruct(seed.shape, jnp.float32),
            jax.ShapeDtypeStruct((depth // RATIO, outputs, wide // RATIO), jnp.float32),
            jax.ShapeDtypeStruct((3, 3, outputs, 6 * inputs), jnp.float32),
        ),
        in_specs=[IN_VMEM] * 5,
        out_specs=[IN_VMEM] * 3,
        scratch_shapes=[
            pltpu.VMEM((depth, 6 * inputs, (height + 2) * wide), jnp.bfloat16),
            pltpu.VMEM((depth + 2, 2 * outputs, height * wide), jnp.bfloat16),
            pltpu.VMEM(seed.shape, jnp.float32),
        ],
        compiler_params=pltpu.CompilerParams(vmem_limit_bytes=48 << 20),
    )(whole, faces, edges, jnp.concatenate([weight, weight], axis=1), seed)
    return hidden, means, gradient[..., : 3 * inputs] + gradient[..., 3 * inputs :]


def as_rows(*arrays):
    return jnp.concatenate([array.reshape(-1, LANES) for array in arrays])


def local(
    sizes,
    fine_in,
    context_in,
    weight_fine,
    weight_coarse,
    lift_weight,
    lower_weight,
    block_row,
    tile_count,
    fine_cotangent,
    coarse_cotangent,
):
    rows_total, columns_total, cores = sizes
    column_here, row_here, core_here = (lax.axis_index(a) for a in ("gx", "gy", "col"))
    column_rows = lax.dynamic_slice_in_dim(block_row, column_here, 1, 1)[:, 0]
    column_counts = lax.dynamic_slice_in_dim(tile_count, column_here, 1, 1)[:, 0].astype(
        jnp.float32
    )
    target = lax.dynamic_slice_in_dim(column_rows, row_here, 1, 0)[0]
    own_count = lax.dynamic_slice_in_dim(column_counts, row_here, 1, 0)[0]
    routed_here = (column_rows == row_here).astype(jnp.float32)
    weights_here = routed_here * column_counts
    divisor_here = jnp.maximum(jnp.sum(weights_here), 1.0)
    divisor_target = jnp.maximum(
        jnp.sum(jnp.where(column_rows == target, column_counts, 0.0)), 1.0
    )
    channels, depth, height, wide = fine_in.shape
    broad, low, short, narrow = context_in.shape
    fine_cells = depth * height * rows_total * wide * columns_total
    coarse_cells = low * short * rows_total * narrow * columns_total
    fine_seed = fine_cotangent * fine_cells ** (-0.5)
    coarse_seed_own = coarse_cotangent * coarse_cells ** (-0.5)
    group_seed = jnp.sum(group_view(fine_seed), axis=(2, 4, 6))

    fine_rows = fine_in.transpose(1, 2, 0, 3)
    edges = jnp.stack([fine_in[..., 0], fine_in[..., wide - 1]])
    near = as_rows(context_in, edges)
    line = as_rows(coarse_seed_own, group_seed, lift_weight, lower_weight)
    whole, faces, nears, lines = opening(sizes, fine_rows, near, line)

    keys = near_keys(rows_total, columns_total)
    context_rows = context_in.size // LANES
    contexts = nears[:, :, :context_rows].reshape(
        len(keys), cores * broad, low, short, narrow
    )
    sides = nears[:, :, context_rows:].reshape(len(keys), cores, 2, channels, depth, height)

    def inside(a, b):
        row, column = row_here + a, column_here + b
        return (row >= 0) & (row < rows_total) & (column >= 0) & (column < columns_total)

    def key(a, b):
        return keys.index((a % rows_total, b % columns_total))

    def kept(a, b, value):
        return value if a == 0 and b == 0 else jnp.where(inside(a, b), value, 0.0)

    def context_piece(a, b):
        block = contexts[key(a, b)]
        block = block[:, :, -1:] if a < 0 else block[:, :, :1] if a > 0 else block
        block = block[..., -1:] if b < 0 else block[..., :1] if b > 0 else block
        return kept(a, b, block)

    coarse_pad = pad_depth(
        jnp.concatenate(
            [
                jnp.concatenate([context_piece(a, b) for b in (-1, 0, 1)], axis=3)
                for a in (-1, 0, 1)
            ],
            axis=2,
        )
    )

    def edge_piece(a, b):
        edge = sides[key(a, b), :, 1 if b < 0 else 0].reshape(cores * channels, depth, height)
        edge = edge[:, :, -1:] if a < 0 else edge[:, :, :1] if a > 0 else edge
        return kept(a, b, edge)

    def edge_column(b):
        column = jnp.concatenate([edge_piece(a, b) for a in (-1, 0, 1)], axis=2)
        return column.transpose(1, 0, 2)

    edge_columns = jnp.stack([edge_column(-1), edge_column(1)])
    known = jnp.stack([inside(-1, 0), inside(1, 0)])[:, None, None, None, None]
    faces = jnp.where(known, faces, 0.0)

    first = coarse_cotangent.size // LANES
    second = first + group_seed.size // LANES
    third = second + lift_weight.size // LANES
    seeds = lines[:, :, :first].reshape(rows_total, cores * broad, low, short, narrow)
    groups = lines[:, :, first:second].reshape(
        rows_total, cores * channels, low, short, narrow
    )
    weights_all = lax.dynamic_index_in_dim(lines, row_here, 0, False)
    lift_all = weights_all[:, second:third].reshape(cores, *lift_weight.shape)
    lower_all = weights_all[:, third:].reshape(cores, *lower_weight.shape)

    lifted_seed_all = jnp.einsum("r,rfzyx->fzyx", routed_here, groups, precision=lax.Precision.HIGHEST)
    lifted_seed = lax.dynamic_slice_in_dim(lifted_seed_all, core_here * channels, channels, 0)
    lift_own = lax.dynamic_slice_in_dim(lift_all, core_here * broad, broad, 1)
    coarse_total_seed = coarse_seed_own + jnp.einsum(
        "kcf,kfzyx->czyx",
        lift_own,
        lifted_seed_all.reshape(cores, channels, low, short, narrow),
        precision=precise,
    )
    lower_own = lax.dynamic_slice_in_dim(lower_all, core_here * channels, channels, 1)
    target_seed = lax.dynamic_index_in_dim(seeds, target, 0, False)
    tile_seed = jnp.einsum(
        "kfc,kczyx->fzyx",
        lower_own,
        target_seed.reshape(cores, broad, low, short, narrow),
        precision=precise,
    ) * (own_count / (RATIO * RATIO * RATIO) / divisor_target)

    coarse_pre = convolve(coarse_pad, weight_coarse)
    coarse_hidden = jax.nn.silu(coarse_pre)
    hidden_seed = fine_seed + refine(tile_seed)
    fine_hidden, tile_means, fine_terms = fine_pass(
        whole,
        faces,
        edge_columns,
        weight_fine,
        hidden_seed.transpose(1, 0, 2, 3).reshape(depth, channels, height * wide),
    )
    fine_hidden = fine_hidden.reshape(depth, channels, height, wide).transpose(1, 0, 2, 3)
    tile_means = tile_means.transpose(1, 0, 2)[:, :, None]
    middle = line_gather(sizes, as_rows(coarse_hidden, tile_means))
    hiddens = middle[:, :, :first].reshape(rows_total, cores * broad, low, short, narrow)
    means = middle[:, :, first:].reshape(rows_total, cores * channels, low, short, narrow)
    coarse_wide = lax.dynamic_index_in_dim(hiddens, row_here, 0, False)
    chosen = jnp.einsum(
        "czyx,cf->fzyx",
        lax.dynamic_index_in_dim(hiddens, target, 0, False),
        lift_weight,
        precision=precise,
    )
    joined_fine = fine_hidden + refine(chosen)
    averaged_wide = (
        jnp.einsum("r,rfzyx->fzyx", weights_here, means, precision=lax.Precision.HIGHEST) / divisor_here
    )
    joined_coarse = coarse_hidden + jnp.einsum(
        "fzyx,fc->czyx", averaged_wide, lower_weight, precision=precise
    )
    lower_gradient = jnp.einsum("fzyx,czyx->fc", averaged_wide, coarse_seed_own, precision=precise)
    lift_gradient = jnp.einsum("czyx,fzyx->cf", coarse_wide, lifted_seed, precision=precise)
    coarse_gradient = kernel_terms(coarse_pad, coarse_total_seed * silu_slope(coarse_pre))
    fine_terms, coarse_gradient, lift_gradient, lower_gradient = total_over_tiles(
        sizes, (fine_terms, coarse_gradient, lift_gradient, lower_gradient)
    )
    fine_gradient = fine_terms.reshape(3, 3, channels, 3, -1).transpose(0, 1, 3, 4, 2)
    return (
        joined_fine,
        joined_coarse,
        fine_gradient,
        coarse_gradient,
        lift_gradient,
        lower_gradient,
    )


def solution(mesh):
    sizes = tuple(mesh.shape[axis] for axis in AXES)
    in_specs = (
        P("col", "grp", "gy", "gx"),
        P("col", "grp", "gy", "gx"),
        P(None, None, None, None, "col"),
        P(None, None, None, None, "col"),
        P(None, "col"),
        P(None, "col"),
        P("grp", None),
        P("grp", None),
        P("col", "grp", "gy", "gx"),
        P("col", "grp", "gy", "gx"),
    )
    out_specs = (
        P("col", "grp", "gy", "gx"),
        P("col", "grp", "gy", "gx"),
        P("grp", None, None, None, "col"),
        P("grp", None, None, None, "col"),
        P("grp", "col"),
        P("grp", "col"),
    )
    return jax.shard_map(
        functools.partial(local, sizes),
        mesh=mesh,
        in_specs=in_specs,
        out_specs=out_specs,
        check_vma=False,
    )
```

```python
import functools

import jax
import jax.numpy as jnp
from jax import lax
from jax.experimental import pallas as pl
from jax.experimental.pallas import tpu as pltpu
from jax.sharding import PartitionSpec as P

RATIO = 4


precise = lax.Precision.HIGH


def pad_depth(volume):
    return jnp.pad(volume, ((0, 0), (1, 1), (0, 0), (0, 0)))


def shifted_stack(padded, shift_z, shift_y, extent_z, extent_y, extent_x):
    return jnp.stack(
        [
            padded[
                :,
                shift_z : shift_z + extent_z,
                shift_y : shift_y + extent_y,
                shift_x : shift_x + extent_x,
            ]
            for shift_x in range(3)
        ]
    )


def convolve(padded, kernel):
    extent_z = padded.shape[1] - 2
    extent_y = padded.shape[2] - 2
    extent_x = padded.shape[3] - 2
    result = jnp.zeros((kernel.shape[4], extent_z, extent_y, extent_x), jnp.float32)
    for shift_z in range(3):
        for shift_y in range(3):
            stacked = shifted_stack(padded, shift_z, shift_y, extent_z, extent_y, extent_x)
            result = result + jnp.einsum(
                "aizyx,aio->ozyx", stacked, kernel[shift_z, shift_y], precision=precise
            )
    return result


def kernel_terms(padded, seed):
    extent_z = seed.shape[1]
    extent_y = seed.shape[2]
    extent_x = seed.shape[3]
    layers_z = []
    for shift_z in range(3):
        layers_y = []
        for shift_y in range(3):
            stacked = shifted_stack(padded, shift_z, shift_y, extent_z, extent_y, extent_x)
            layers_y.append(jnp.einsum("aizyx,ozyx->aio", stacked, seed, precision=precise))
        layers_z.append(jnp.stack(layers_y))
    return jnp.stack(layers_z)


def silu_slope(value):
    logistic = jax.nn.sigmoid(value)
    return logistic * (1.0 + value * (1.0 - logistic))


def refine(block):
    channels, extent_z, extent_y, extent_x = block.shape
    grown = jnp.broadcast_to(
        block[:, :, None, :, None, :, None],
        (channels, extent_z, RATIO, extent_y, RATIO, extent_x, RATIO),
    )
    return grown.reshape(channels, extent_z * RATIO, extent_y * RATIO, extent_x * RATIO)


def group_view(volume):
    channels, extent_z, extent_y, extent_x = volume.shape
    return volume.reshape(
        channels, extent_z // RATIO, RATIO, extent_y // RATIO, RATIO, extent_x // RATIO, RATIO
    )


LANES = 128
AXES = ("gy", "gx", "col")
MESH = pl.DeviceIdType.MESH
IN_VMEM = pl.BlockSpec(memory_space=pltpu.VMEM)


def near_keys(rows, columns):
    return sorted({(a % rows, b % columns) for a in (-1, 0, 1) for b in (-1, 0, 1)})


def peer(sizes, offset):
    return {
        axis: lax.rem(lax.axis_index(axis) + step, size) if step else lax.axis_index(axis)
        for axis, size, step in zip(AXES, sizes, offset)
    }


def greet(sizes, offsets):
    barrier = pltpu.get_barrier_semaphore()
    for offset in offsets:
        pl.semaphore_signal(barrier, inc=1, device_id=peer(sizes, offset), device_id_type=MESH)
    pl.semaphore_wait(barrier, len(offsets))


def spread(sizes, kinds):
    rows, columns, cores = sizes
    assert cores == 2
    plan = []
    if "face" in kinds:
        plan += [("last", (1, 0, 0)), ("first", (rows - 1, 0, 0))]
    if "line" in kinds:
        plan += [
            ("line", (a, b, 0)) for a in range(rows) for b in range(columns) if (a, b) != (0, 0)
        ]
    if "near" in kinds:
        plan += [("near", (a, b, 0)) for a, b in near_keys(rows, columns) if (a, b) != (0, 0)]
    return plan


def both_ways(sizes, plan):
    found = {offset for _, offset in plan} | {(0, 0, 1)}
    found |= {tuple((n - s) % n for n, s in zip(sizes, offset)) for offset in found}
    return sorted(found)


def remote(source, goal, send, recv, target):
    return pltpu.make_async_remote_copy(
        src_ref=source,
        dst_ref=goal,
        send_sem=send,
        recv_sem=recv,
        device_id=target,
        device_id_type=MESH,
    )


def opening_kernel(
    sizes, fine, near, line, extra, whole_out, face_out, near_out, line_out, extra_out,
    send, recv, send_on, recv_on, send_own, recv_own,
):
    rows, columns, _ = sizes
    plan = spread(sizes, ("face", "line", "near"))
    keys = near_keys(rows, columns)
    row_here, column_here, core_here = (lax.axis_index(axis) for axis in AXES)
    greet(sizes, both_ways(sizes, plan))
    height = fine.shape[1]
    other = peer(sizes, (0, 0, 1))
    not_last, not_first = row_here < rows - 1, row_here > 0
    always = None

    def guarded(condition, action):
        if condition is always:
            action()
        else:
            pl.when(condition)(action)

    steps = []
    for index, (kind, offset) in enumerate(plan):
        sends = gets = always
        if kind == "last":
            source, goal, landed = fine.at[:, height - 1], face_out.at[0, core_here], None
            sends, gets = not_last, not_first
        elif kind == "first":
            source, goal, landed = fine.at[:, 0], face_out.at[1, core_here], None
            sends, gets = not_first, not_last
        elif kind == "near":
            slot = keys.index(((rows - offset[0]) % rows, (columns - offset[1]) % columns))
            source, goal, landed = near, near_out.at[slot, core_here], None
        else:
            source, goal = line, line_out.at[row_here, column_here, core_here]
            origin = peer(sizes, ((rows - offset[0]) % rows, (columns - offset[1]) % columns, 0))
            landed = line_out.at[origin["gy"], origin["gx"], core_here]
        landed = goal if landed is None else landed
        copy = remote(source, goal, send.at[index], recv.at[index], peer(sizes, offset))
        onward = remote(landed, landed, send_on.at[index], recv_on.at[index], other)
        guarded(sends, copy.start)
        steps.append((copy, onward, sends, gets))
    own = [
        (near, near_out.at[keys.index((0, 0)), core_here]),
        (line, line_out.at[row_here, column_here, core_here]),
        (extra, extra_out.at[core_here]),
        (fine, whole_out.at[core_here]),
    ]
    own = [
        remote(source, goal, send_own.at[index], recv_own.at[index], other)
        for index, (source, goal) in enumerate(own)
    ]
    for copy in own:
        copy.start()
    near_out[keys.index((0, 0)), core_here] = near[...]
    line_out[row_here, column_here, core_here] = line[...]
    extra_out[core_here] = extra[...]
    whole_out[core_here] = fine[...]

    def clear(side):
        face_out[side] = jnp.zeros(face_out.shape[1:], face_out.dtype)

    pl.when(row_here == 0)(lambda: clear(0))
    pl.when(row_here == rows - 1)(lambda: clear(1))
    for copy, onward, _, gets in steps[2:] + steps[:2]:

        def forward(copy=copy, onward=onward):
            copy.wait_recv()
            onward.start()

        guarded(gets, forward)
    for copy, onward, sends, gets in steps:
        guarded(sends, copy.wait_send)
        guarded(gets, onward.wait)
    for copy in own:
        copy.wait()


def opening(sizes, fine, near, line, extra):
    rows, columns, cores = sizes
    number = len(spread(sizes, ("face", "line", "near")))
    depth, _, channels, wide = fine.shape
    return pl.pallas_call(
        functools.partial(opening_kernel, sizes),
        out_shape=(
            jax.ShapeDtypeStruct((cores, *fine.shape), jnp.float32),
            jax.ShapeDtypeStruct((2, cores, depth, channels, wide), jnp.float32),
            jax.ShapeDtypeStruct((len(near_keys(rows, columns)), cores, *near.shape), jnp.float32),
            jax.ShapeDtypeStruct((rows, columns, cores, *line.shape), jnp.float32),
            jax.ShapeDtypeStruct((cores, *extra.shape), jnp.float32),
        ),
        in_specs=[IN_VMEM] * 4,
        out_specs=[IN_VMEM] * 5,
        scratch_shapes=[pltpu.SemaphoreType.DMA((number,))] * 4
        + [pltpu.SemaphoreType.DMA((4,))] * 2,
        compiler_params=pltpu.CompilerParams(
            collective_id=0, has_side_effects=True, vmem_limit_bytes=48 << 20
        ),
    )(fine, near, line, extra)


def closing_kernel(
    sizes, parts, line, result, line_out, landed,
    send, recv, send_back, recv_back, send_line, recv_line, send_on, recv_on, send_own, recv_own,
):
    rows, columns, _ = sizes
    plan = spread(sizes, ("line",))
    offsets = [offset for _, offset in plan]
    row_here, column_here, core_here = (lax.axis_index(axis) for axis in AXES)
    here = row_here * columns + column_here
    greet(sizes, both_ways(sizes, plan))
    other = peer(sizes, (0, 0, 1))
    own_line = line_out.at[row_here, column_here, core_here]
    first, lines = [], []
    for index, offset in enumerate(offsets):
        target = peer(sizes, offset)
        place = target["gy"] * columns + target["gx"]
        first.append(
            remote(parts.at[place], landed.at[index], send.at[index], recv.at[index], target)
        )
        first[-1].start()
    for index, offset in enumerate(offsets):
        origin = peer(sizes, ((rows - offset[0]) % rows, (columns - offset[1]) % columns, 0))
        arrived = line_out.at[origin["gy"], origin["gx"], core_here]
        copy = remote(line, own_line, send_line.at[index], recv_line.at[index], peer(sizes, offset))
        lines.append((copy, remote(arrived, arrived, send_on.at[index], recv_on.at[index], other)))
        copy.start()
    own = remote(line, own_line, send_own.at[0], recv_own.at[0], other)
    own.start()
    line_out[row_here, column_here, core_here] = line[...]
    total = parts[here]
    for index, copy in enumerate(first):
        copy.wait()
        total = total + landed[index]
    result[here] = total
    back = []
    for index, offset in enumerate(offsets):
        back.append(
            remote(
                result.at[here],
                result.at[here],
                send_back.at[index],
                recv_back.at[index],
                peer(sizes, offset),
            )
        )
        back[-1].start()
    for copy, onward in lines:
        copy.wait_recv()
        onward.start()
    for copy, onward in lines:
        copy.wait_send()
        onward.wait()
    own.wait()
    for copy in back:
        copy.wait()


def closing(sizes, arrays, line):
    rows, columns, cores = sizes
    peers = rows * columns
    flat = jnp.concatenate([array.reshape(-1, LANES) for array in arrays])
    chunk = -(-flat.shape[0] // (8 * peers)) * 8
    parts = jnp.pad(flat, ((0, peers * chunk - flat.shape[0]), (0, 0))).reshape(peers, chunk, LANES)
    number = peers - 1
    result, lines = pl.pallas_call(
        functools.partial(closing_kernel, sizes),
        out_shape=(
            jax.ShapeDtypeStruct(parts.shape, jnp.float32),
            jax.ShapeDtypeStruct((rows, columns, cores, *line.shape), jnp.float32),
        ),
        in_specs=[IN_VMEM] * 2,
        out_specs=[IN_VMEM] * 2,
        scratch_shapes=[pltpu.VMEM((number, chunk, LANES), jnp.float32)]
        + [pltpu.SemaphoreType.DMA((number,))] * 8
        + [pltpu.SemaphoreType.DMA((1,))] * 2,
        compiler_params=pltpu.CompilerParams(collective_id=1, has_side_effects=True),
    )(parts, line)
    result = result.reshape(peers * chunk, LANES)
    given, start = [], 0
    for array in arrays:
        count = array.size // LANES
        given.append(result[start : start + count].reshape(array.shape))
        start += count
    return given, lines


def halves(value):
    high = value.astype(jnp.bfloat16)
    return high, (value - high.astype(jnp.float32)).astype(jnp.bfloat16)


def fine_kernel(whole, faces, edges, weight, seed, hidden, means, gradient, taps, slopes, sums):
    cores, depth, height, channels, wide = whole.shape
    inputs = cores * channels
    outputs = seed.shape[1]
    span = height * wide
    lanes = lax.broadcasted_iota(jnp.int32, (inputs, wide), 1)
    weight_all = jnp.concatenate(halves(weight[...]), axis=0)
    half = weight_all.shape[0] // 2
    for z in (0, depth + 1):
        slopes[z] = jnp.zeros(slopes.shape[1:], slopes.dtype)
    pooled = []

    def finish(z):
        value = sums[z]
        logistic = jax.nn.sigmoid(value)
        active = value * logistic
        hidden[z] = active
        high, rest = halves(seed[z] * (logistic * (1.0 + value * (1.0 - logistic))))
        slopes[z + 1, :outputs] = high
        slopes[z + 1, outputs:] = rest
        rows = sum(active[:, y * wide : (y + 1) * wide] for y in range(height))
        if z % RATIO == 0:
            pooled.append(rows)
        else:
            pooled[-1] = pooled[-1] + rows

    for z in range(depth):
        for y in range(height + 2):
            if y == 0:
                row = faces[0, :, z]
            elif y == height + 1:
                row = faces[1, :, z]
            else:
                row = whole[:, z, y - 1]
            row = row.reshape(inputs, wide)
            left = jnp.where(lanes == 0, edges[0, z][:, y : y + 1], pltpu.roll(row, 1, 1))
            right = jnp.where(
                lanes == wide - 1, edges[1, z][:, y : y + 1], pltpu.roll(row, wide - 1, 1)
            )
            high, rest = halves(jnp.concatenate([left, row, right], axis=0))
            place = slice(y * wide, (y + 1) * wide)
            taps[z, : 3 * inputs, place] = high
            taps[z, 3 * inputs :, place] = rest
        product = jnp.dot(weight_all, taps[z], preferred_element_type=jnp.float32)
        for dz in range(3):
            goal = z - dz + 1
            if not 0 <= goal < depth:
                continue
            term = None
            for dy in range(3):
                at = (dz * 3 + dy) * outputs
                for start in (at, half + at):
                    piece = product[start : start + outputs, dy * wide : dy * wide + span]
                    term = piece if term is None else term + piece
            sums[goal] = term if z == max(goal - 1, 0) else sums[goal] + term
        if z:
            finish(z - 1)
    finish(depth - 1)
    groups = wide // RATIO
    pool = (
        lax.broadcasted_iota(jnp.int32, (wide, groups), 0) // RATIO
        == lax.broadcasted_iota(jnp.int32, (wide, groups), 1)
    ).astype(jnp.float32)
    for index, rows in enumerate(pooled):
        means[index] = jnp.dot(
            rows, pool, precision=lax.Precision.HIGHEST, preferred_element_type=jnp.float32
        ) * (1.0 / RATIO**3)
    for dy in range(3):
        total = None
        for z in range(depth):
            term = lax.dot_general(
                slopes[z : z + 3].reshape(6 * outputs, span),
                taps[z, :, dy * wide : dy * wide + span],
                (((1,), (1,)), ((), ())),
                preferred_element_type=jnp.float32,
            )
            total = term if total is None else total + term
        for place in range(3):
            at = place * 2 * outputs
            gradient[2 - place, dy] = (
                total[at : at + outputs] + total[at + outputs : at + 2 * outputs]
            )


def fine_pass(whole, faces, edges, weight_fine, seed):
    cores, depth, height, channels, wide = whole.shape
    inputs, outputs = weight_fine.shape[3:]
    weight = weight_fine.transpose(0, 1, 4, 2, 3).reshape(9 * outputs, 3 * inputs)
    hidden, means, gradient = pl.pallas_call(
        fine_kernel,
        out_shape=(
            jax.ShapeDtypeStruct(seed.shape, jnp.float32),
            jax.ShapeDtypeStruct((depth // RATIO, outputs, wide // RATIO), jnp.float32),
            jax.ShapeDtypeStruct((3, 3, outputs, 6 * inputs), jnp.float32),
        ),
        in_specs=[IN_VMEM] * 5,
        out_specs=[IN_VMEM] * 3,
        scratch_shapes=[
            pltpu.VMEM((depth, 6 * inputs, (height + 2) * wide), jnp.bfloat16),
            pltpu.VMEM((depth + 2, 2 * outputs, height * wide), jnp.bfloat16),
            pltpu.VMEM(seed.shape, jnp.float32),
        ],
        compiler_params=pltpu.CompilerParams(vmem_limit_bytes=48 << 20),
    )(whole, faces, edges, jnp.concatenate([weight, weight], axis=1), seed)
    return hidden, means, gradient[..., : 3 * inputs] + gradient[..., 3 * inputs :]


def as_rows(*arrays):
    return jnp.concatenate([array.reshape(-1, LANES) for array in arrays])


def local(
    sizes,
    fine_in,
    context_in,
    weight_fine,
    weight_coarse,
    lift_weight,
    lower_weight,
    block_row,
    tile_count,
    fine_cotangent,
    coarse_cotangent,
):
    rows_total, columns_total, cores = sizes
    column_here, row_here, core_here = (lax.axis_index(a) for a in ("gx", "gy", "col"))
    column_rows = lax.dynamic_slice_in_dim(block_row, column_here, 1, 1)[:, 0]
    column_counts = lax.dynamic_slice_in_dim(tile_count, column_here, 1, 1)[:, 0].astype(
        jnp.float32
    )
    target = lax.dynamic_slice_in_dim(column_rows, row_here, 1, 0)[0]
    own_count = lax.dynamic_slice_in_dim(column_counts, row_here, 1, 0)[0]
    every_row = jnp.arange(rows_total, dtype=jnp.int32)
    routed = (block_row[None] == every_row[:, None, None]).astype(jnp.float32)
    weighted = routed * tile_count.astype(jnp.float32)[None]
    divisors = jnp.maximum(jnp.sum(weighted, axis=1), 1.0)
    divisor_target = jnp.maximum(
        jnp.sum(jnp.where(column_rows == target, column_counts, 0.0)), 1.0
    )
    channels, depth, height, wide = fine_in.shape
    broad, low, short, narrow = context_in.shape
    fine_cells = depth * height * rows_total * wide * columns_total
    coarse_cells = low * short * rows_total * narrow * columns_total
    fine_seed = fine_cotangent * fine_cells ** (-0.5)
    coarse_seed_own = coarse_cotangent * coarse_cells ** (-0.5)
    group_seed = jnp.sum(group_view(fine_seed), axis=(2, 4, 6))

    fine_rows = fine_in.transpose(1, 2, 0, 3)
    edges = jnp.stack([fine_in[..., 0], fine_in[..., wide - 1]])
    near = as_rows(context_in, edges)
    line = as_rows(coarse_seed_own, group_seed)
    extra = as_rows(lift_weight, lower_weight)
    whole, faces, nears, lines, extras = opening(sizes, fine_rows, near, line, extra)

    keys = near_keys(rows_total, columns_total)
    context_rows = context_in.size // LANES
    contexts = nears[:, :, :context_rows].reshape(
        len(keys), cores * broad, low, short, narrow
    )
    sides = nears[:, :, context_rows:].reshape(len(keys), cores, 2, channels, depth, height)

    def inside(a, b):
        row, column = row_here + a, column_here + b
        return (row >= 0) & (row < rows_total) & (column >= 0) & (column < columns_total)

    def key(a, b):
        return keys.index((a % rows_total, b % columns_total))

    def kept(a, b, value):
        return value if a == 0 and b == 0 else jnp.where(inside(a, b), value, 0.0)

    def context_piece(a, b):
        block = contexts[key(a, b)]
        block = block[:, :, -1:] if a < 0 else block[:, :, :1] if a > 0 else block
        block = block[..., -1:] if b < 0 else block[..., :1] if b > 0 else block
        return kept(a, b, block)

    coarse_pad = pad_depth(
        jnp.concatenate(
            [
                jnp.concatenate([context_piece(a, b) for b in (-1, 0, 1)], axis=3)
                for a in (-1, 0, 1)
            ],
            axis=2,
        )
    )

    def edge_piece(a, b):
        edge = sides[key(a, b), :, 1 if b < 0 else 0].reshape(cores * channels, depth, height)
        edge = edge[:, :, -1:] if a < 0 else edge[:, :, :1] if a > 0 else edge
        return kept(a, b, edge)

    def edge_column(b):
        column = jnp.concatenate([edge_piece(a, b) for a in (-1, 0, 1)], axis=2)
        return column.transpose(1, 0, 2)

    edge_columns = jnp.stack([edge_column(-1), edge_column(1)])

    first = coarse_cotangent.size // LANES
    lift_rows = lift_weight.size // LANES
    line_shape = (rows_total, columns_total)
    seeds = lines[:, :, :, :first].reshape(*line_shape, cores, broad, low, short, narrow)
    groups = lines[:, :, :, first:].reshape(*line_shape, cores * channels, low, short, narrow)
    lift_all = extras[:, :lift_rows].reshape(cores, *lift_weight.shape)
    lower_all = extras[:, lift_rows:].reshape(cores, *lower_weight.shape)

    def routed_sum(factors, values):
        factors = factors.reshape(*factors.shape, 1, 1, 1, 1)
        return jnp.sum(factors * values[None], axis=1)

    def block_at(values, row):
        return lax.dynamic_index_in_dim(
            lax.dynamic_index_in_dim(values, row, 0, False), column_here, 0, False
        )

    lifted_seeds = routed_sum(routed, groups)
    lifted_seed_all = block_at(lifted_seeds, row_here)
    lifted_seeds_own = lax.dynamic_slice_in_dim(lifted_seeds, core_here * channels, channels, 2)
    seeds_own = lax.dynamic_index_in_dim(seeds, core_here, 2, False)
    lift_own = lax.dynamic_slice_in_dim(lift_all, core_here * broad, broad, 1)
    coarse_total_seed = coarse_seed_own + jnp.einsum(
        "kcf,kfzyx->czyx",
        lift_own,
        lifted_seed_all.reshape(cores, channels, low, short, narrow),
        precision=precise,
    )
    lower_own = lax.dynamic_slice_in_dim(lower_all, core_here * channels, channels, 1)
    target_seed = block_at(seeds, target)
    tile_seed = jnp.einsum(
        "kfc,kczyx->fzyx",
        lower_own,
        target_seed,
        precision=precise,
    ) * (own_count / (RATIO * RATIO * RATIO) / divisor_target)

    coarse_pre = convolve(coarse_pad, weight_coarse)
    coarse_hidden = jax.nn.silu(coarse_pre)
    hidden_seed = fine_seed + refine(tile_seed)
    fine_hidden, tile_means, fine_terms = fine_pass(
        whole,
        faces,
        edge_columns,
        weight_fine,
        hidden_seed.transpose(1, 0, 2, 3).reshape(depth, channels, height * wide),
    )
    fine_hidden = fine_hidden.reshape(depth, channels, height, wide).transpose(1, 0, 2, 3)
    tile_means = tile_means.transpose(1, 0, 2)[:, :, None]
    coarse_gradient = kernel_terms(coarse_pad, coarse_total_seed * silu_slope(coarse_pre))
    (fine_terms, coarse_gradient), middle = closing(
        sizes, (fine_terms, coarse_gradient), as_rows(coarse_hidden, tile_means)
    )
    hiddens = middle[:, :, :, :first].reshape(*line_shape, cores * broad, low, short, narrow)
    means = middle[:, :, :, first:].reshape(*line_shape, cores * channels, low, short, narrow)
    chosen = jnp.einsum(
        "czyx,cf->fzyx", block_at(hiddens, target), lift_weight, precision=precise
    )
    joined_fine = fine_hidden + refine(chosen)
    averaged = routed_sum(weighted, means) / divisors[:, :, None, None, None, None]
    joined_coarse = coarse_hidden + jnp.einsum(
        "fzyx,fc->czyx", block_at(averaged, row_here), lower_weight, precision=precise
    )
    lower_gradient = jnp.einsum("kifzyx,kiczyx->fc", averaged, seeds_own, precision=precise)
    lift_gradient = jnp.einsum("kiczyx,kifzyx->cf", hiddens, lifted_seeds_own, precision=precise)
    fine_gradient = fine_terms.reshape(3, 3, channels, 3, -1).transpose(0, 1, 3, 4, 2)
    return (
        joined_fine,
        joined_coarse,
        fine_gradient,
        coarse_gradient,
        lift_gradient,
        lower_gradient,
    )


def solution(mesh):
    sizes = tuple(mesh.shape[axis] for axis in AXES)
    in_specs = (
        P("col", "grp", "gy", "gx"),
        P("col", "grp", "gy", "gx"),
        P(None, None, None, None, "col"),
        P(None, None, None, None, "col"),
        P(None, "col"),
        P(None, "col"),
        P("grp", None),
        P("grp", None),
        P("col", "grp", "gy", "gx"),
        P("col", "grp", "gy", "gx"),
    )
    out_specs = (
        P("col", "grp", "gy", "gx"),
        P("col", "grp", "gy", "gx"),
        P("grp", None, None, None, "col"),
        P("grp", None, None, None, "col"),
        P("grp", "col"),
        P("grp", "col"),
    )
    return jax.shard_map(
        functools.partial(local, sizes),
        mesh=mesh,
        in_specs=in_specs,
        out_specs=out_specs,
        check_vma=False,
    )
```

```python
import functools

import jax
import jax.numpy as jnp
from jax import lax
from jax.experimental import pallas as pl
from jax.experimental.pallas import tpu as pltpu
from jax.sharding import PartitionSpec as P

RATIO = 4


precise = lax.Precision.HIGH


def pad_depth(volume):
    return jnp.pad(volume, ((0, 0), (1, 1), (0, 0), (0, 0)))


def shifted_stack(padded, shift_z, shift_y, extent_z, extent_y, extent_x):
    return jnp.stack(
        [
            padded[
                :,
                shift_z : shift_z + extent_z,
                shift_y : shift_y + extent_y,
                shift_x : shift_x + extent_x,
            ]
            for shift_x in range(3)
        ]
    )


def convolve(padded, kernel):
    extent_z = padded.shape[1] - 2
    extent_y = padded.shape[2] - 2
    extent_x = padded.shape[3] - 2
    result = jnp.zeros((kernel.shape[4], extent_z, extent_y, extent_x), jnp.float32)
    for shift_z in range(3):
        for shift_y in range(3):
            stacked = shifted_stack(padded, shift_z, shift_y, extent_z, extent_y, extent_x)
            result = result + jnp.einsum(
                "aizyx,aio->ozyx", stacked, kernel[shift_z, shift_y], precision=precise
            )
    return result


def kernel_terms(padded, seed):
    extent_z = seed.shape[1]
    extent_y = seed.shape[2]
    extent_x = seed.shape[3]
    layers_z = []
    for shift_z in range(3):
        layers_y = []
        for shift_y in range(3):
            stacked = shifted_stack(padded, shift_z, shift_y, extent_z, extent_y, extent_x)
            layers_y.append(jnp.einsum("aizyx,ozyx->aio", stacked, seed, precision=precise))
        layers_z.append(jnp.stack(layers_y))
    return jnp.stack(layers_z)


def silu_slope(value):
    logistic = jax.nn.sigmoid(value)
    return logistic * (1.0 + value * (1.0 - logistic))


def refine(block):
    channels, extent_z, extent_y, extent_x = block.shape
    grown = jnp.broadcast_to(
        block[:, :, None, :, None, :, None],
        (channels, extent_z, RATIO, extent_y, RATIO, extent_x, RATIO),
    )
    return grown.reshape(channels, extent_z * RATIO, extent_y * RATIO, extent_x * RATIO)


def group_view(volume):
    channels, extent_z, extent_y, extent_x = volume.shape
    return volume.reshape(
        channels, extent_z // RATIO, RATIO, extent_y // RATIO, RATIO, extent_x // RATIO, RATIO
    )


LANES = 128
AXES = ("gy", "gx", "col")
MESH = pl.DeviceIdType.MESH
IN_VMEM = pl.BlockSpec(memory_space=pltpu.VMEM)


def near_keys(rows, columns):
    return sorted({(a % rows, b % columns) for a in (-1, 0, 1) for b in (-1, 0, 1)})


def peer(sizes, offset):
    return {
        axis: lax.rem(lax.axis_index(axis) + step, size) if step else lax.axis_index(axis)
        for axis, size, step in zip(AXES, sizes, offset)
    }


def greet(sizes, offsets):
    barrier = pltpu.get_barrier_semaphore()
    for offset in offsets:
        pl.semaphore_signal(barrier, inc=1, device_id=peer(sizes, offset), device_id_type=MESH)
    pl.semaphore_wait(barrier, len(offsets))


def spread(sizes, kinds):
    rows, columns, cores = sizes
    assert cores == 2
    plan = []
    if "face" in kinds:
        plan += [("last", (1, 0, 0)), ("first", (rows - 1, 0, 0))]
    if "line" in kinds:
        plan += [
            ("line", (a, b, 0)) for a in range(rows) for b in range(columns) if (a, b) != (0, 0)
        ]
    if "near" in kinds:
        plan += [("near", (a, b, 0)) for a, b in near_keys(rows, columns) if (a, b) != (0, 0)]
    return plan


def both_ways(sizes, plan):
    found = {offset for _, offset in plan} | {(0, 0, 1)}
    found |= {tuple((n - s) % n for n, s in zip(sizes, offset)) for offset in found}
    return sorted(found)


def remote(source, goal, send, recv, target):
    return pltpu.make_async_remote_copy(
        src_ref=source,
        dst_ref=goal,
        send_sem=send,
        recv_sem=recv,
        device_id=target,
        device_id_type=MESH,
    )


def opening_kernel(
    sizes, fine, near, line, extra, whole_out, face_out, near_out, line_out, extra_out,
    send, recv, send_on, recv_on, send_own, recv_own,
):
    rows, columns, _ = sizes
    plan = spread(sizes, ("face", "line", "near"))
    keys = near_keys(rows, columns)
    row_here, column_here, core_here = (lax.axis_index(axis) for axis in AXES)
    greet(sizes, both_ways(sizes, plan))
    height = fine.shape[1]
    other = peer(sizes, (0, 0, 1))
    not_last, not_first = row_here < rows - 1, row_here > 0
    always = None

    def guarded(condition, action):
        if condition is always:
            action()
        else:
            pl.when(condition)(action)

    steps = []
    for index, (kind, offset) in enumerate(plan):
        sends = gets = always
        if kind == "last":
            source, goal, landed = fine.at[:, height - 1], face_out.at[0, core_here], None
            sends, gets = not_last, not_first
        elif kind == "first":
            source, goal, landed = fine.at[:, 0], face_out.at[1, core_here], None
            sends, gets = not_first, not_last
        elif kind == "near":
            slot = keys.index(((rows - offset[0]) % rows, (columns - offset[1]) % columns))
            source, goal, landed = near, near_out.at[slot, core_here], None
        else:
            source, goal = line, line_out.at[row_here, column_here, core_here]
            origin = peer(sizes, ((rows - offset[0]) % rows, (columns - offset[1]) % columns, 0))
            landed = line_out.at[origin["gy"], origin["gx"], core_here]
        landed = goal if landed is None else landed
        copy = remote(source, goal, send.at[index], recv.at[index], peer(sizes, offset))
        onward = remote(landed, landed, send_on.at[index], recv_on.at[index], other)
        guarded(sends, copy.start)
        steps.append((copy, onward, sends, gets))
    own = [
        (near, near_out.at[keys.index((0, 0)), core_here]),
        (line, line_out.at[row_here, column_here, core_here]),
        (extra, extra_out.at[core_here]),
        (fine, whole_out.at[core_here]),
    ]
    own = [
        remote(source, goal, send_own.at[index], recv_own.at[index], other)
        for index, (source, goal) in enumerate(own)
    ]
    for copy in own:
        copy.start()
    near_out[keys.index((0, 0)), core_here] = near[...]
    line_out[row_here, column_here, core_here] = line[...]
    extra_out[core_here] = extra[...]
    whole_out[core_here] = fine[...]

    def clear(side):
        face_out[side] = jnp.zeros(face_out.shape[1:], face_out.dtype)

    pl.when(row_here == 0)(lambda: clear(0))
    pl.when(row_here == rows - 1)(lambda: clear(1))
    for copy, onward, _, gets in steps[2:] + steps[:2]:

        def forward(copy=copy, onward=onward):
            copy.wait_recv()
            onward.start()

        guarded(gets, forward)
    for copy, onward, sends, gets in steps:
        guarded(sends, copy.wait_send)
        guarded(gets, onward.wait)
    for copy in own:
        copy.wait()


def opening(sizes, fine, near, line, extra):
    rows, columns, cores = sizes
    number = len(spread(sizes, ("face", "line", "near")))
    depth, _, channels, wide = fine.shape
    return pl.pallas_call(
        functools.partial(opening_kernel, sizes),
        out_shape=(
            jax.ShapeDtypeStruct((cores, *fine.shape), jnp.float32),
            jax.ShapeDtypeStruct((2, cores, depth, channels, wide), jnp.float32),
            jax.ShapeDtypeStruct((len(near_keys(rows, columns)), cores, *near.shape), jnp.float32),
            jax.ShapeDtypeStruct((rows, columns, cores, *line.shape), jnp.float32),
            jax.ShapeDtypeStruct((cores, *extra.shape), jnp.float32),
        ),
        in_specs=[IN_VMEM] * 4,
        out_specs=[IN_VMEM] * 5,
        scratch_shapes=[pltpu.SemaphoreType.DMA((number,))] * 4
        + [pltpu.SemaphoreType.DMA((4,))] * 2,
        compiler_params=pltpu.CompilerParams(
            collective_id=0, has_side_effects=True, vmem_limit_bytes=48 << 20
        ),
    )(fine, near, line, extra)


def closing_kernel(
    sizes, parts, line, result, line_out, landed_x, outgoing, landed_z,
    send_x, recv_x, send_z, recv_z, back_z, got_z, back_x, got_x, send_line, recv_line, send_on, recv_on, send_own, recv_own,
):
    rows, columns, _ = sizes
    plan = spread(sizes, ("line",))
    offsets = [offset for _, offset in plan]
    row_here, column_here, core_here = (lax.axis_index(axis) for axis in AXES)
    here = row_here * columns + column_here
    greet(sizes, both_ways(sizes, plan))
    other = peer(sizes, (0, 0, 1))
    own_line = line_out.at[row_here, column_here, core_here]
    lines = []
    across = columns - 1
    order = list(range(1, rows)) + [0]

    def place(a, column):
        return lax.rem(row_here + a, rows) * columns + column

    sideways = {}
    for a in order:
        for b in range(1, columns):
            index = a * across + b - 1
            target = peer(sizes, (0, b, 0))
            sideways[a, b] = remote(
                parts.at[place(a, target["gx"])],
                landed_x.at[index],
                send_x.at[index],
                recv_x.at[index],
                target,
            )
            sideways[a, b].start()
    for index, offset in enumerate(offsets):
        origin = peer(sizes, ((rows - offset[0]) % rows, (columns - offset[1]) % columns, 0))
        arrived = line_out.at[origin["gy"], origin["gx"], core_here]
        copy = remote(line, own_line, send_line.at[index], recv_line.at[index], peer(sizes, offset))
        lines.append((copy, remote(arrived, arrived, send_on.at[index], recv_on.at[index], other)))
        copy.start()
    own = remote(line, own_line, send_own.at[0], recv_own.at[0], other)
    own.start()
    line_out[row_here, column_here, core_here] = line[...]
    along = []
    for a in order:
        total = parts[place(a, column_here)]
        for b in range(1, columns):
            sideways[a, b].wait()
            total = total + landed_x[a * across + b - 1]
        if a:
            outgoing[a - 1] = total
            along.append(
                remote(
                    outgoing.at[a - 1],
                    landed_z.at[a - 1],
                    send_z.at[a - 1],
                    recv_z.at[a - 1],
                    peer(sizes, (a, 0, 0)),
                )
            )
            along[-1].start()
    for index, copy in enumerate(along):
        copy.wait()
        total = total + landed_z[index]
    result[here] = total
    back, wide = [], []

    def pass_sideways(a):
        for b in range(1, columns):
            index = a * across + b - 1
            piece = result.at[place(rows - a, column_here)]
            wide.append(
                remote(piece, piece, back_x.at[index], got_x.at[index], peer(sizes, (0, b, 0)))
            )
            wide[-1].start()

    for a in range(1, rows):
        piece = result.at[here]
        back.append(
            remote(piece, piece, back_z.at[a - 1], got_z.at[a - 1], peer(sizes, (a, 0, 0)))
        )
        back[-1].start()
    pass_sideways(0)
    for a in range(1, rows):
        back[a - 1].wait_recv()
        pass_sideways(a)
    for copy, onward in lines:
        copy.wait_recv()
        onward.start()
    for copy, onward in lines:
        copy.wait_send()
        onward.wait()
    own.wait()
    for copy in back:
        copy.wait_send()
    for copy in wide:
        copy.wait()


def closing(sizes, arrays, line):
    rows, columns, cores = sizes
    peers = rows * columns
    flat = jnp.concatenate([array.reshape(-1, LANES) for array in arrays])
    chunk = -(-flat.shape[0] // (8 * peers)) * 8
    parts = jnp.pad(flat, ((0, peers * chunk - flat.shape[0]), (0, 0))).reshape(peers, chunk, LANES)
    number = peers - 1
    result, lines = pl.pallas_call(
        functools.partial(closing_kernel, sizes),
        out_shape=(
            jax.ShapeDtypeStruct(parts.shape, jnp.float32),
            jax.ShapeDtypeStruct((rows, columns, cores, *line.shape), jnp.float32),
        ),
        in_specs=[IN_VMEM] * 2,
        out_specs=[IN_VMEM] * 2,
        scratch_shapes=[
            pltpu.VMEM((rows * (columns - 1), chunk, LANES), jnp.float32),
            pltpu.VMEM((rows - 1, chunk, LANES), jnp.float32),
            pltpu.VMEM((rows - 1, chunk, LANES), jnp.float32),
        ]
        + [pltpu.SemaphoreType.DMA((rows * (columns - 1),))] * 2
        + [pltpu.SemaphoreType.DMA((rows - 1,))] * 4
        + [pltpu.SemaphoreType.DMA((rows * (columns - 1),))] * 2
        + [pltpu.SemaphoreType.DMA((number,))] * 4
        + [pltpu.SemaphoreType.DMA((1,))] * 2,
        compiler_params=pltpu.CompilerParams(collective_id=1, has_side_effects=True),
    )(parts, line)
    result = result.reshape(peers * chunk, LANES)
    given, start = [], 0
    for array in arrays:
        count = array.size // LANES
        given.append(result[start : start + count].reshape(array.shape))
        start += count
    return given, lines


def halves(value):
    high = value.astype(jnp.bfloat16)
    return high, (value - high.astype(jnp.float32)).astype(jnp.bfloat16)


def fine_kernel(whole, faces, edges, weight, seed, hidden, means, gradient, taps, slopes, sums):
    cores, depth, height, channels, wide = whole.shape
    inputs = cores * channels
    outputs = seed.shape[1]
    span = height * wide
    lanes = lax.broadcasted_iota(jnp.int32, (inputs, wide), 1)
    weight_all = jnp.concatenate(halves(weight[...]), axis=0)
    half = weight_all.shape[0] // 2
    for z in (0, depth + 1):
        slopes[z] = jnp.zeros(slopes.shape[1:], slopes.dtype)
    pooled = []

    def finish(z):
        value = sums[z]
        logistic = jax.nn.sigmoid(value)
        active = value * logistic
        hidden[z] = active
        high, rest = halves(seed[z] * (logistic * (1.0 + value * (1.0 - logistic))))
        slopes[z + 1, :outputs] = high
        slopes[z + 1, outputs:] = rest
        rows = sum(active[:, y * wide : (y + 1) * wide] for y in range(height))
        if z % RATIO == 0:
            pooled.append(rows)
        else:
            pooled[-1] = pooled[-1] + rows

    for z in range(depth):
        for y in range(height + 2):
            if y == 0:
                row = faces[0, :, z]
            elif y == height + 1:
                row = faces[1, :, z]
            else:
                row = whole[:, z, y - 1]
            row = row.reshape(inputs, wide)
            left = jnp.where(lanes == 0, edges[0, z][:, y : y + 1], pltpu.roll(row, 1, 1))
            right = jnp.where(
                lanes == wide - 1, edges[1, z][:, y : y + 1], pltpu.roll(row, wide - 1, 1)
            )
            high, rest = halves(jnp.concatenate([left, row, right], axis=0))
            place = slice(y * wide, (y + 1) * wide)
            taps[z, : 3 * inputs, place] = high
            taps[z, 3 * inputs :, place] = rest
        product = jnp.dot(weight_all, taps[z], preferred_element_type=jnp.float32)
        for dz in range(3):
            goal = z - dz + 1
            if not 0 <= goal < depth:
                continue
            term = None
            for dy in range(3):
                at = (dz * 3 + dy) * outputs
                for start in (at, half + at):
                    piece = product[start : start + outputs, dy * wide : dy * wide + span]
                    term = piece if term is None else term + piece
            sums[goal] = term if z == max(goal - 1, 0) else sums[goal] + term
        if z:
            finish(z - 1)
    finish(depth - 1)
    groups = wide // RATIO
    pool = (
        lax.broadcasted_iota(jnp.int32, (wide, groups), 0) // RATIO
        == lax.broadcasted_iota(jnp.int32, (wide, groups), 1)
    ).astype(jnp.float32)
    for index, rows in enumerate(pooled):
        means[index] = jnp.dot(
            rows, pool, precision=lax.Precision.HIGHEST, preferred_element_type=jnp.float32
        ) * (1.0 / RATIO**3)
    for dy in range(3):
        total = None
        for z in range(depth):
            term = lax.dot_general(
                slopes[z : z + 3].reshape(6 * outputs, span),
                taps[z, :, dy * wide : dy * wide + span],
                (((1,), (1,)), ((), ())),
                preferred_element_type=jnp.float32,
            )
            total = term if total is None else total + term
        for place in range(3):
            at = place * 2 * outputs
            gradient[2 - place, dy] = (
                total[at : at + outputs] + total[at + outputs : at + 2 * outputs]
            )


def fine_pass(whole, faces, edges, weight_fine, seed):
    cores, depth, height, channels, wide = whole.shape
    inputs, outputs = weight_fine.shape[3:]
    weight = weight_fine.transpose(0, 1, 4, 2, 3).reshape(9 * outputs, 3 * inputs)
    hidden, means, gradient = pl.pallas_call(
        fine_kernel,
        out_shape=(
            jax.ShapeDtypeStruct(seed.shape, jnp.float32),
            jax.ShapeDtypeStruct((depth // RATIO, outputs, wide // RATIO), jnp.float32),
            jax.ShapeDtypeStruct((3, 3, outputs, 6 * inputs), jnp.float32),
        ),
        in_specs=[IN_VMEM] * 5,
        out_specs=[IN_VMEM] * 3,
        scratch_shapes=[
            pltpu.VMEM((depth, 6 * inputs, (height + 2) * wide), jnp.bfloat16),
            pltpu.VMEM((depth + 2, 2 * outputs, height * wide), jnp.bfloat16),
            pltpu.VMEM(seed.shape, jnp.float32),
        ],
        compiler_params=pltpu.CompilerParams(vmem_limit_bytes=48 << 20),
    )(whole, faces, edges, jnp.concatenate([weight, weight], axis=1), seed)
    return hidden, means, gradient[..., : 3 * inputs] + gradient[..., 3 * inputs :]


def as_rows(*arrays):
    return jnp.concatenate([array.reshape(-1, LANES) for array in arrays])


def local(
    sizes,
    fine_in,
    context_in,
    weight_fine,
    weight_coarse,
    lift_weight,
    lower_weight,
    block_row,
    tile_count,
    fine_cotangent,
    coarse_cotangent,
):
    rows_total, columns_total, cores = sizes
    column_here, row_here, core_here = (lax.axis_index(a) for a in ("gx", "gy", "col"))
    column_rows = lax.dynamic_slice_in_dim(block_row, column_here, 1, 1)[:, 0]
    column_counts = lax.dynamic_slice_in_dim(tile_count, column_here, 1, 1)[:, 0].astype(
        jnp.float32
    )
    target = lax.dynamic_slice_in_dim(column_rows, row_here, 1, 0)[0]
    own_count = lax.dynamic_slice_in_dim(column_counts, row_here, 1, 0)[0]
    every_row = jnp.arange(rows_total, dtype=jnp.int32)
    routed = (block_row[None] == every_row[:, None, None]).astype(jnp.float32)
    weighted = routed * tile_count.astype(jnp.float32)[None]
    divisors = jnp.maximum(jnp.sum(weighted, axis=1), 1.0)
    divisor_target = jnp.maximum(
        jnp.sum(jnp.where(column_rows == target, column_counts, 0.0)), 1.0
    )
    channels, depth, height, wide = fine_in.shape
    broad, low, short, narrow = context_in.shape
    fine_cells = depth * height * rows_total * wide * columns_total
    coarse_cells = low * short * rows_total * narrow * columns_total
    fine_seed = fine_cotangent * fine_cells ** (-0.5)
    coarse_seed_own = coarse_cotangent * coarse_cells ** (-0.5)
    group_seed = jnp.sum(group_view(fine_seed), axis=(2, 4, 6))

    fine_rows = fine_in.transpose(1, 2, 0, 3)
    edges = jnp.stack([fine_in[..., 0], fine_in[..., wide - 1]])
    near = as_rows(context_in, edges)
    line = as_rows(coarse_seed_own, group_seed)
    extra = as_rows(lift_weight, lower_weight)
    whole, faces, nears, lines, extras = opening(sizes, fine_rows, near, line, extra)

    keys = near_keys(rows_total, columns_total)
    context_rows = context_in.size // LANES
    contexts = nears[:, :, :context_rows].reshape(
        len(keys), cores * broad, low, short, narrow
    )
    sides = nears[:, :, context_rows:].reshape(len(keys), cores, 2, channels, depth, height)

    def inside(a, b):
        row, column = row_here + a, column_here + b
        return (row >= 0) & (row < rows_total) & (column >= 0) & (column < columns_total)

    def key(a, b):
        return keys.index((a % rows_total, b % columns_total))

    def kept(a, b, value):
        return value if a == 0 and b == 0 else jnp.where(inside(a, b), value, 0.0)

    def context_piece(a, b):
        block = contexts[key(a, b)]
        block = block[:, :, -1:] if a < 0 else block[:, :, :1] if a > 0 else block
        block = block[..., -1:] if b < 0 else block[..., :1] if b > 0 else block
        return kept(a, b, block)

    coarse_pad = pad_depth(
        jnp.concatenate(
            [
                jnp.concatenate([context_piece(a, b) for b in (-1, 0, 1)], axis=3)
                for a in (-1, 0, 1)
            ],
            axis=2,
        )
    )

    def edge_piece(a, b):
        edge = sides[key(a, b), :, 1 if b < 0 else 0].reshape(cores * channels, depth, height)
        edge = edge[:, :, -1:] if a < 0 else edge[:, :, :1] if a > 0 else edge
        return kept(a, b, edge)

    def edge_column(b):
        column = jnp.concatenate([edge_piece(a, b) for a in (-1, 0, 1)], axis=2)
        return column.transpose(1, 0, 2)

    edge_columns = jnp.stack([edge_column(-1), edge_column(1)])

    first = coarse_cotangent.size // LANES
    lift_rows = lift_weight.size // LANES
    line_shape = (rows_total, columns_total)
    seeds = lines[:, :, :, :first].reshape(*line_shape, cores, broad, low, short, narrow)
    groups = lines[:, :, :, first:].reshape(*line_shape, cores * channels, low, short, narrow)
    lift_all = extras[:, :lift_rows].reshape(cores, *lift_weight.shape)
    lower_all = extras[:, lift_rows:].reshape(cores, *lower_weight.shape)

    def routed_sum(factors, values):
        factors = factors.reshape(*factors.shape, 1, 1, 1, 1)
        return jnp.sum(factors * values[None], axis=1)

    def block_at(values, row):
        return lax.dynamic_index_in_dim(
            lax.dynamic_index_in_dim(values, row, 0, False), column_here, 0, False
        )

    lifted_seeds = routed_sum(routed, groups)
    lifted_seed_all = block_at(lifted_seeds, row_here)
    lifted_seeds_own = lax.dynamic_slice_in_dim(lifted_seeds, core_here * channels, channels, 2)
    seeds_own = lax.dynamic_index_in_dim(seeds, core_here, 2, False)
    lift_own = lax.dynamic_slice_in_dim(lift_all, core_here * broad, broad, 1)
    coarse_total_seed = coarse_seed_own + jnp.einsum(
        "kcf,kfzyx->czyx",
        lift_own,
        lifted_seed_all.reshape(cores, channels, low, short, narrow),
        precision=precise,
    )
    lower_own = lax.dynamic_slice_in_dim(lower_all, core_here * channels, channels, 1)
    target_seed = block_at(seeds, target)
    tile_seed = jnp.einsum(
        "kfc,kczyx->fzyx",
        lower_own,
        target_seed,
        precision=precise,
    ) * (own_count / (RATIO * RATIO * RATIO) / divisor_target)

    coarse_pre = convolve(coarse_pad, weight_coarse)
    coarse_hidden = jax.nn.silu(coarse_pre)
    hidden_seed = fine_seed + refine(tile_seed)
    fine_hidden, tile_means, fine_terms = fine_pass(
        whole,
        faces,
        edge_columns,
        weight_fine,
        hidden_seed.transpose(1, 0, 2, 3).reshape(depth, channels, height * wide),
    )
    fine_hidden = fine_hidden.reshape(depth, channels, height, wide).transpose(1, 0, 2, 3)
    tile_means = tile_means.transpose(1, 0, 2)[:, :, None]
    coarse_gradient = kernel_terms(coarse_pad, coarse_total_seed * silu_slope(coarse_pre))
    (fine_terms, coarse_gradient), middle = closing(
        sizes, (fine_terms, coarse_gradient), as_rows(coarse_hidden, tile_means)
    )
    hiddens = middle[:, :, :, :first].reshape(*line_shape, cores * broad, low, short, narrow)
    means = middle[:, :, :, first:].reshape(*line_shape, cores * channels, low, short, narrow)
    chosen = jnp.einsum(
        "czyx,cf->fzyx", block_at(hiddens, target), lift_weight, precision=precise
    )
    joined_fine = fine_hidden + refine(chosen)
    averaged = routed_sum(weighted, means) / divisors[:, :, None, None, None, None]
    joined_coarse = coarse_hidden + jnp.einsum(
        "fzyx,fc->czyx", block_at(averaged, row_here), lower_weight, precision=precise
    )
    lower_gradient = jnp.einsum("kifzyx,kiczyx->fc", averaged, seeds_own, precision=precise)
    lift_gradient = jnp.einsum("kiczyx,kifzyx->cf", hiddens, lifted_seeds_own, precision=precise)
    fine_gradient = fine_terms.reshape(3, 3, channels, 3, -1).transpose(0, 1, 3, 4, 2)
    return (
        joined_fine,
        joined_coarse,
        fine_gradient,
        coarse_gradient,
        lift_gradient,
        lower_gradient,
    )


def solution(mesh):
    sizes = tuple(mesh.shape[axis] for axis in AXES)
    in_specs = (
        P("col", "grp", "gy", "gx"),
        P("col", "grp", "gy", "gx"),
        P(None, None, None, None, "col"),
        P(None, None, None, None, "col"),
        P(None, "col"),
        P(None, "col"),
        P("grp", None),
        P("grp", None),
        P("col", "grp", "gy", "gx"),
        P("col", "grp", "gy", "gx"),
    )
    out_specs = (
        P("col", "grp", "gy", "gx"),
        P("col", "grp", "gy", "gx"),
        P("grp", None, None, None, "col"),
        P("grp", None, None, None, "col"),
        P("grp", "col"),
        P("grp", "col"),
    )
    return jax.shard_map(
        functools.partial(local, sizes),
        mesh=mesh,
        in_specs=in_specs,
        out_specs=out_specs,
        check_vma=False,
    )
```

```python
import functools

import jax
import jax.numpy as jnp
from jax import lax
from jax.experimental import pallas as pl
from jax.experimental.pallas import tpu as pltpu
from jax.sharding import PartitionSpec as P

RATIO = 4


precise = lax.Precision.HIGH


def pad_depth(volume):
    return jnp.pad(volume, ((0, 0), (1, 1), (0, 0), (0, 0)))


def shifted_stack(padded, shift_z, shift_y, extent_z, extent_y, extent_x):
    return jnp.stack(
        [
            padded[
                :,
                shift_z : shift_z + extent_z,
                shift_y : shift_y + extent_y,
                shift_x : shift_x + extent_x,
            ]
            for shift_x in range(3)
        ]
    )


def convolve(padded, kernel):
    extent_z = padded.shape[1] - 2
    extent_y = padded.shape[2] - 2
    extent_x = padded.shape[3] - 2
    result = jnp.zeros((kernel.shape[4], extent_z, extent_y, extent_x), jnp.float32)
    for shift_z in range(3):
        for shift_y in range(3):
            stacked = shifted_stack(padded, shift_z, shift_y, extent_z, extent_y, extent_x)
            result = result + jnp.einsum(
                "aizyx,aio->ozyx", stacked, kernel[shift_z, shift_y], precision=precise
            )
    return result


def kernel_terms(padded, seed):
    extent_z = seed.shape[1]
    extent_y = seed.shape[2]
    extent_x = seed.shape[3]
    layers_z = []
    for shift_z in range(3):
        layers_y = []
        for shift_y in range(3):
            stacked = shifted_stack(padded, shift_z, shift_y, extent_z, extent_y, extent_x)
            layers_y.append(jnp.einsum("aizyx,ozyx->aio", stacked, seed, precision=precise))
        layers_z.append(jnp.stack(layers_y))
    return jnp.stack(layers_z)


def silu_slope(value):
    logistic = jax.nn.sigmoid(value)
    return logistic * (1.0 + value * (1.0 - logistic))


def refine(block):
    channels, extent_z, extent_y, extent_x = block.shape
    grown = jnp.broadcast_to(
        block[:, :, None, :, None, :, None],
        (channels, extent_z, RATIO, extent_y, RATIO, extent_x, RATIO),
    )
    return grown.reshape(channels, extent_z * RATIO, extent_y * RATIO, extent_x * RATIO)


def group_view(volume):
    channels, extent_z, extent_y, extent_x = volume.shape
    return volume.reshape(
        channels, extent_z // RATIO, RATIO, extent_y // RATIO, RATIO, extent_x // RATIO, RATIO
    )


LANES = 128
AXES = ("gy", "gx", "col")
MESH = pl.DeviceIdType.MESH
IN_VMEM = pl.BlockSpec(memory_space=pltpu.VMEM)


def near_keys(rows, columns):
    return sorted({(a % rows, b % columns) for a in (-1, 0, 1) for b in (-1, 0, 1)})


def peer(sizes, offset):
    return {
        axis: lax.rem(lax.axis_index(axis) + step, size) if step else lax.axis_index(axis)
        for axis, size, step in zip(AXES, sizes, offset)
    }


def greet(sizes, offsets):
    barrier = pltpu.get_barrier_semaphore()
    for offset in offsets:
        pl.semaphore_signal(barrier, inc=1, device_id=peer(sizes, offset), device_id_type=MESH)
    pl.semaphore_wait(barrier, len(offsets))


def spread(sizes, kinds):
    rows, columns, cores = sizes
    assert cores == 2
    plan = []
    if "face" in kinds:
        plan += [("last", (1, 0, 0)), ("first", (rows - 1, 0, 0))]
    if "line" in kinds:
        plan += [
            ("line", (a, b, 0)) for a in range(rows) for b in range(columns) if (a, b) != (0, 0)
        ]
    if "near" in kinds:
        plan += [("near", (a, b, 0)) for a, b in near_keys(rows, columns) if (a, b) != (0, 0)]
    return plan


def both_ways(sizes, plan):
    found = {offset for _, offset in plan} | {(0, 0, 1)}
    found |= {tuple((n - s) % n for n, s in zip(sizes, offset)) for offset in found}
    return sorted(found)


def remote(source, goal, send, recv, target):
    return pltpu.make_async_remote_copy(
        src_ref=source,
        dst_ref=goal,
        send_sem=send,
        recv_sem=recv,
        device_id=target,
        device_id_type=MESH,
    )


def opening_kernel(
    sizes, fine, near, line, extra, whole_out, face_out, near_out, line_out, extra_out,
    send, recv, send_on, recv_on, send_own, recv_own,
):
    rows, columns, _ = sizes
    plan = spread(sizes, ("face", "line", "near"))
    keys = near_keys(rows, columns)
    row_here, column_here, core_here = (lax.axis_index(axis) for axis in AXES)
    greet(sizes, both_ways(sizes, plan))
    height = fine.shape[1]
    other = peer(sizes, (0, 0, 1))
    not_last, not_first = row_here < rows - 1, row_here > 0
    always = None

    def guarded(condition, action):
        if condition is always:
            action()
        else:
            pl.when(condition)(action)

    steps = []
    for index, (kind, offset) in enumerate(plan):
        sends = gets = always
        if kind == "last":
            source, goal, landed = fine.at[:, height - 1], face_out.at[0, core_here], None
            sends, gets = not_last, not_first
        elif kind == "first":
            source, goal, landed = fine.at[:, 0], face_out.at[1, core_here], None
            sends, gets = not_first, not_last
        elif kind == "near":
            slot = keys.index(((rows - offset[0]) % rows, (columns - offset[1]) % columns))
            source, goal, landed = near, near_out.at[slot, core_here], None
        else:
            source, goal = line, line_out.at[row_here, column_here, core_here]
            origin = peer(sizes, ((rows - offset[0]) % rows, (columns - offset[1]) % columns, 0))
            landed = line_out.at[origin["gy"], origin["gx"], core_here]
        landed = goal if landed is None else landed
        copy = remote(source, goal, send.at[index], recv.at[index], peer(sizes, offset))
        onward = remote(landed, landed, send_on.at[index], recv_on.at[index], other)
        guarded(sends, copy.start)
        steps.append((copy, onward, sends, gets))
    own = [
        (near, near_out.at[keys.index((0, 0)), core_here]),
        (line, line_out.at[row_here, column_here, core_here]),
        (extra, extra_out.at[core_here]),
        (fine, whole_out.at[core_here]),
    ]
    own = [
        remote(source, goal, send_own.at[index], recv_own.at[index], other)
        for index, (source, goal) in enumerate(own)
    ]
    for copy in own:
        copy.start()
    near_out[keys.index((0, 0)), core_here] = near[...]
    line_out[row_here, column_here, core_here] = line[...]
    extra_out[core_here] = extra[...]
    whole_out[core_here] = fine[...]

    def clear(side):
        face_out[side] = jnp.zeros(face_out.shape[1:], face_out.dtype)

    pl.when(row_here == 0)(lambda: clear(0))
    pl.when(row_here == rows - 1)(lambda: clear(1))
    for copy, onward, _, gets in steps[2:] + steps[:2]:

        def forward(copy=copy, onward=onward):
            copy.wait_recv()
            onward.start()

        guarded(gets, forward)
    for copy, onward, sends, gets in steps:
        guarded(sends, copy.wait_send)
        guarded(gets, onward.wait)
    for copy in own:
        copy.wait()


def opening(sizes, fine, near, line, extra):
    rows, columns, cores = sizes
    number = len(spread(sizes, ("face", "line", "near")))
    depth, _, channels, wide = fine.shape
    return pl.pallas_call(
        functools.partial(opening_kernel, sizes),
        out_shape=(
            jax.ShapeDtypeStruct((cores, *fine.shape), jnp.float32),
            jax.ShapeDtypeStruct((2, cores, depth, channels, wide), jnp.float32),
            jax.ShapeDtypeStruct((len(near_keys(rows, columns)), cores, *near.shape), jnp.float32),
            jax.ShapeDtypeStruct((rows, columns, cores, *line.shape), jnp.float32),
            jax.ShapeDtypeStruct((cores, *extra.shape), jnp.float32),
        ),
        in_specs=[IN_VMEM] * 4,
        out_specs=[IN_VMEM] * 5,
        scratch_shapes=[pltpu.SemaphoreType.DMA((number,))] * 4
        + [pltpu.SemaphoreType.DMA((4,))] * 2,
        compiler_params=pltpu.CompilerParams(
            collective_id=0, has_side_effects=True, vmem_limit_bytes=48 << 20
        ),
    )(fine, near, line, extra)


def closing_kernel(
    sizes, parts, line, result, line_out, landed,
    send, recv, send_back, recv_back, send_line, recv_line, send_on, recv_on, send_own, recv_own,
):
    rows, columns, _ = sizes
    plan = spread(sizes, ("line",))
    offsets = [offset for _, offset in plan]
    row_here, column_here, core_here = (lax.axis_index(axis) for axis in AXES)
    here = row_here * columns + column_here
    greet(sizes, both_ways(sizes, plan))
    other = peer(sizes, (0, 0, 1))
    own_line = line_out.at[row_here, column_here, core_here]
    first, lines = [], []
    for index, offset in enumerate(offsets):
        origin = peer(sizes, ((rows - offset[0]) % rows, (columns - offset[1]) % columns, 0))
        arrived = line_out.at[origin["gy"], origin["gx"], core_here]
        copy = remote(line, own_line, send_line.at[index], recv_line.at[index], peer(sizes, offset))
        lines.append((copy, remote(arrived, arrived, send_on.at[index], recv_on.at[index], other)))
        copy.start()
    for index, offset in enumerate(offsets):
        target = peer(sizes, offset)
        place = target["gy"] * columns + target["gx"]
        first.append(
            remote(parts.at[place], landed.at[index], send.at[index], recv.at[index], target)
        )
        first[-1].start()
    own = remote(line, own_line, send_own.at[0], recv_own.at[0], other)
    own.start()
    line_out[row_here, column_here, core_here] = line[...]
    for copy, onward in lines:
        copy.wait_recv()
        onward.start()
    total = parts[here]
    for index, copy in enumerate(first):
        copy.wait()
        total = total + landed[index]
    result[here] = total
    back = []
    for index, offset in enumerate(offsets):
        back.append(
            remote(
                result.at[here],
                result.at[here],
                send_back.at[index],
                recv_back.at[index],
                peer(sizes, offset),
            )
        )
        back[-1].start()
    for copy, onward in lines:
        copy.wait_send()
        onward.wait()
    own.wait()
    for copy in back:
        copy.wait()


def closing(sizes, arrays, line):
    rows, columns, cores = sizes
    peers = rows * columns
    flat = jnp.concatenate([array.reshape(-1, LANES) for array in arrays])
    chunk = -(-flat.shape[0] // (8 * peers)) * 8
    parts = jnp.pad(flat, ((0, peers * chunk - flat.shape[0]), (0, 0))).reshape(peers, chunk, LANES)
    number = peers - 1
    result, lines = pl.pallas_call(
        functools.partial(closing_kernel, sizes),
        out_shape=(
            jax.ShapeDtypeStruct(parts.shape, jnp.float32),
            jax.ShapeDtypeStruct((rows, columns, cores, *line.shape), jnp.float32),
        ),
        in_specs=[IN_VMEM] * 2,
        out_specs=[IN_VMEM] * 2,
        scratch_shapes=[pltpu.VMEM((number, chunk, LANES), jnp.float32)]
        + [pltpu.SemaphoreType.DMA((number,))] * 8
        + [pltpu.SemaphoreType.DMA((1,))] * 2,
        compiler_params=pltpu.CompilerParams(collective_id=1, has_side_effects=True),
    )(parts, line)
    result = result.reshape(peers * chunk, LANES)
    given, start = [], 0
    for array in arrays:
        count = array.size // LANES
        given.append(result[start : start + count].reshape(array.shape))
        start += count
    return given, lines


def halves(value):
    high = value.astype(jnp.bfloat16)
    return high, (value - high.astype(jnp.float32)).astype(jnp.bfloat16)


def fine_kernel(whole, faces, edges, weight, seed, hidden, means, gradient, taps, slopes, sums):
    cores, depth, height, channels, wide = whole.shape
    inputs = cores * channels
    outputs = seed.shape[1]
    span = height * wide
    lanes = lax.broadcasted_iota(jnp.int32, (inputs, wide), 1)
    weight_all = jnp.concatenate(halves(weight[...]), axis=0)
    half = weight_all.shape[0] // 2
    for z in (0, depth + 1):
        slopes[z] = jnp.zeros(slopes.shape[1:], slopes.dtype)
    pooled = []

    def finish(z):
        value = sums[z]
        logistic = jax.nn.sigmoid(value)
        active = value * logistic
        hidden[z] = active
        high, rest = halves(seed[z] * (logistic * (1.0 + value * (1.0 - logistic))))
        slopes[z + 1, :outputs] = high
        slopes[z + 1, outputs:] = rest
        rows = sum(active[:, y * wide : (y + 1) * wide] for y in range(height))
        if z % RATIO == 0:
            pooled.append(rows)
        else:
            pooled[-1] = pooled[-1] + rows

    for z in range(depth):
        for y in range(height + 2):
            if y == 0:
                row = faces[0, :, z]
            elif y == height + 1:
                row = faces[1, :, z]
            else:
                row = whole[:, z, y - 1]
            row = row.reshape(inputs, wide)
            left = jnp.where(lanes == 0, edges[0, z][:, y : y + 1], pltpu.roll(row, 1, 1))
            right = jnp.where(
                lanes == wide - 1, edges[1, z][:, y : y + 1], pltpu.roll(row, wide - 1, 1)
            )
            high, rest = halves(jnp.concatenate([left, row, right], axis=0))
            place = slice(y * wide, (y + 1) * wide)
            taps[z, : 3 * inputs, place] = high
            taps[z, 3 * inputs :, place] = rest
        product = jnp.dot(weight_all, taps[z], preferred_element_type=jnp.float32)
        for dz in range(3):
            goal = z - dz + 1
            if not 0 <= goal < depth:
                continue
            term = None
            for dy in range(3):
                at = (dz * 3 + dy) * outputs
                for start in (at, half + at):
                    piece = product[start : start + outputs, dy * wide : dy * wide + span]
                    term = piece if term is None else term + piece
            sums[goal] = term if z == max(goal - 1, 0) else sums[goal] + term
        if z:
            finish(z - 1)
    finish(depth - 1)
    groups = wide // RATIO
    pool = (
        lax.broadcasted_iota(jnp.int32, (wide, groups), 0) // RATIO
        == lax.broadcasted_iota(jnp.int32, (wide, groups), 1)
    ).astype(jnp.float32)
    for index, rows in enumerate(pooled):
        means[index] = jnp.dot(
            rows, pool, precision=lax.Precision.HIGHEST, preferred_element_type=jnp.float32
        ) * (1.0 / RATIO**3)
    for dy in range(3):
        total = None
        for z in range(depth):
            term = lax.dot_general(
                slopes[z : z + 3].reshape(6 * outputs, span),
                taps[z, :, dy * wide : dy * wide + span],
                (((1,), (1,)), ((), ())),
                preferred_element_type=jnp.float32,
            )
            total = term if total is None else total + term
        for place in range(3):
            at = place * 2 * outputs
            gradient[2 - place, dy] = (
                total[at : at + outputs] + total[at + outputs : at + 2 * outputs]
            )


def fine_pass(whole, faces, edges, weight_fine, seed):
    cores, depth, height, channels, wide = whole.shape
    inputs, outputs = weight_fine.shape[3:]
    weight = weight_fine.transpose(0, 1, 4, 2, 3).reshape(9 * outputs, 3 * inputs)
    hidden, means, gradient = pl.pallas_call(
        fine_kernel,
        out_shape=(
            jax.ShapeDtypeStruct(seed.shape, jnp.float32),
            jax.ShapeDtypeStruct((depth // RATIO, outputs, wide // RATIO), jnp.float32),
            jax.ShapeDtypeStruct((3, 3, outputs, 6 * inputs), jnp.float32),
        ),
        in_specs=[IN_VMEM] * 5,
        out_specs=[IN_VMEM] * 3,
        scratch_shapes=[
            pltpu.VMEM((depth, 6 * inputs, (height + 2) * wide), jnp.bfloat16),
            pltpu.VMEM((depth + 2, 2 * outputs, height * wide), jnp.bfloat16),
            pltpu.VMEM(seed.shape, jnp.float32),
        ],
        compiler_params=pltpu.CompilerParams(vmem_limit_bytes=48 << 20),
    )(whole, faces, edges, jnp.concatenate([weight, weight], axis=1), seed)
    return hidden, means, gradient[..., : 3 * inputs] + gradient[..., 3 * inputs :]


def as_rows(*arrays):
    return jnp.concatenate([array.reshape(-1, LANES) for array in arrays])


def local(
    sizes,
    fine_in,
    context_in,
    weight_fine,
    weight_coarse,
    lift_weight,
    lower_weight,
    block_row,
    tile_count,
    fine_cotangent,
    coarse_cotangent,
):
    rows_total, columns_total, cores = sizes
    column_here, row_here, core_here = (lax.axis_index(a) for a in ("gx", "gy", "col"))
    column_rows = lax.dynamic_slice_in_dim(block_row, column_here, 1, 1)[:, 0]
    column_counts = lax.dynamic_slice_in_dim(tile_count, column_here, 1, 1)[:, 0].astype(
        jnp.float32
    )
    target = lax.dynamic_slice_in_dim(column_rows, row_here, 1, 0)[0]
    own_count = lax.dynamic_slice_in_dim(column_counts, row_here, 1, 0)[0]
    every_row = jnp.arange(rows_total, dtype=jnp.int32)
    routed = (block_row[None] == every_row[:, None, None]).astype(jnp.float32)
    weighted = routed * tile_count.astype(jnp.float32)[None]
    divisors = jnp.maximum(jnp.sum(weighted, axis=1), 1.0)
    divisor_target = jnp.maximum(
        jnp.sum(jnp.where(column_rows == target, column_counts, 0.0)), 1.0
    )
    channels, depth, height, wide = fine_in.shape
    broad, low, short, narrow = context_in.shape
    fine_cells = depth * height * rows_total * wide * columns_total
    coarse_cells = low * short * rows_total * narrow * columns_total
    fine_seed = fine_cotangent * fine_cells ** (-0.5)
    coarse_seed_own = coarse_cotangent * coarse_cells ** (-0.5)
    group_seed = jnp.sum(group_view(fine_seed), axis=(2, 4, 6))

    fine_rows = fine_in.transpose(1, 2, 0, 3)
    edges = jnp.stack([fine_in[..., 0], fine_in[..., wide - 1]])
    near = as_rows(context_in, edges)
    line = as_rows(coarse_seed_own, group_seed)
    extra = as_rows(lift_weight, lower_weight)
    whole, faces, nears, lines, extras = opening(sizes, fine_rows, near, line, extra)

    keys = near_keys(rows_total, columns_total)
    context_rows = context_in.size // LANES
    contexts = nears[:, :, :context_rows].reshape(
        len(keys), cores * broad, low, short, narrow
    )
    sides = nears[:, :, context_rows:].reshape(len(keys), cores, 2, channels, depth, height)

    def inside(a, b):
        row, column = row_here + a, column_here + b
        return (row >= 0) & (row < rows_total) & (column >= 0) & (column < columns_total)

    def key(a, b):
        return keys.index((a % rows_total, b % columns_total))

    def kept(a, b, value):
        return value if a == 0 and b == 0 else jnp.where(inside(a, b), value, 0.0)

    def context_piece(a, b):
        block = contexts[key(a, b)]
        block = block[:, :, -1:] if a < 0 else block[:, :, :1] if a > 0 else block
        block = block[..., -1:] if b < 0 else block[..., :1] if b > 0 else block
        return kept(a, b, block)

    coarse_pad = pad_depth(
        jnp.concatenate(
            [
                jnp.concatenate([context_piece(a, b) for b in (-1, 0, 1)], axis=3)
                for a in (-1, 0, 1)
            ],
            axis=2,
        )
    )

    def edge_piece(a, b):
        edge = sides[key(a, b), :, 1 if b < 0 else 0].reshape(cores * channels, depth, height)
        edge = edge[:, :, -1:] if a < 0 else edge[:, :, :1] if a > 0 else edge
        return kept(a, b, edge)

    def edge_column(b):
        column = jnp.concatenate([edge_piece(a, b) for a in (-1, 0, 1)], axis=2)
        return column.transpose(1, 0, 2)

    edge_columns = jnp.stack([edge_column(-1), edge_column(1)])

    first = coarse_cotangent.size // LANES
    lift_rows = lift_weight.size // LANES
    line_shape = (rows_total, columns_total)
    seeds = lines[:, :, :, :first].reshape(*line_shape, cores, broad, low, short, narrow)
    groups = lines[:, :, :, first:].reshape(*line_shape, cores * channels, low, short, narrow)
    lift_all = extras[:, :lift_rows].reshape(cores, *lift_weight.shape)
    lower_all = extras[:, lift_rows:].reshape(cores, *lower_weight.shape)

    def routed_sum(factors, values):
        factors = factors.reshape(*factors.shape, 1, 1, 1, 1)
        return jnp.sum(factors * values[None], axis=1)

    def block_at(values, row):
        return lax.dynamic_index_in_dim(
            lax.dynamic_index_in_dim(values, row, 0, False), column_here, 0, False
        )

    lifted_seeds = routed_sum(routed, groups)
    lifted_seed_all = block_at(lifted_seeds, row_here)
    lifted_seeds_own = lax.dynamic_slice_in_dim(lifted_seeds, core_here * channels, channels, 2)
    seeds_own = lax.dynamic_index_in_dim(seeds, core_here, 2, False)
    lift_own = lax.dynamic_slice_in_dim(lift_all, core_here * broad, broad, 1)
    coarse_total_seed = coarse_seed_own + jnp.einsum(
        "kcf,kfzyx->czyx",
        lift_own,
        lifted_seed_all.reshape(cores, channels, low, short, narrow),
        precision=precise,
    )
    lower_own = lax.dynamic_slice_in_dim(lower_all, core_here * channels, channels, 1)
    target_seed = block_at(seeds, target)
    tile_seed = jnp.einsum(
        "kfc,kczyx->fzyx",
        lower_own,
        target_seed,
        precision=precise,
    ) * (own_count / (RATIO * RATIO * RATIO) / divisor_target)

    coarse_pre = convolve(coarse_pad, weight_coarse)
    coarse_hidden = jax.nn.silu(coarse_pre)
    hidden_seed = fine_seed + refine(tile_seed)
    fine_hidden, tile_means, fine_terms = fine_pass(
        whole,
        faces,
        edge_columns,
        weight_fine,
        hidden_seed.transpose(1, 0, 2, 3).reshape(depth, channels, height * wide),
    )
    fine_hidden = fine_hidden.reshape(depth, channels, height, wide).transpose(1, 0, 2, 3)
    tile_means = tile_means.transpose(1, 0, 2)[:, :, None]
    coarse_gradient = kernel_terms(coarse_pad, coarse_total_seed * silu_slope(coarse_pre))
    (fine_terms, coarse_gradient), middle = closing(
        sizes, (fine_terms, coarse_gradient), as_rows(coarse_hidden, tile_means)
    )
    hiddens = middle[:, :, :, :first].reshape(*line_shape, cores * broad, low, short, narrow)
    means = middle[:, :, :, first:].reshape(*line_shape, cores * channels, low, short, narrow)
    chosen = jnp.einsum(
        "czyx,cf->fzyx", block_at(hiddens, target), lift_weight, precision=precise
    )
    joined_fine = fine_hidden + refine(chosen)
    averaged = routed_sum(weighted, means) / divisors[:, :, None, None, None, None]
    joined_coarse = coarse_hidden + jnp.einsum(
        "fzyx,fc->czyx", block_at(averaged, row_here), lower_weight, precision=precise
    )
    lower_gradient = jnp.einsum("kifzyx,kiczyx->fc", averaged, seeds_own, precision=precise)
    lift_gradient = jnp.einsum("kiczyx,kifzyx->cf", hiddens, lifted_seeds_own, precision=precise)
    fine_gradient = fine_terms.reshape(3, 3, channels, 3, -1).transpose(0, 1, 3, 4, 2)
    return (
        joined_fine,
        joined_coarse,
        fine_gradient,
        coarse_gradient,
        lift_gradient,
        lower_gradient,
    )


def solution(mesh):
    sizes = tuple(mesh.shape[axis] for axis in AXES)
    in_specs = (
        P("col", "grp", "gy", "gx"),
        P("col", "grp", "gy", "gx"),
        P(None, None, None, None, "col"),
        P(None, None, None, None, "col"),
        P(None, "col"),
        P(None, "col"),
        P("grp", None),
        P("grp", None),
        P("col", "grp", "gy", "gx"),
        P("col", "grp", "gy", "gx"),
    )
    out_specs = (
        P("col", "grp", "gy", "gx"),
        P("col", "grp", "gy", "gx"),
        P("grp", None, None, None, "col"),
        P("grp", None, None, None, "col"),
        P("grp", "col"),
        P("grp", "col"),
    )
    return jax.shard_map(
        functools.partial(local, sizes),
        mesh=mesh,
        in_specs=in_specs,
        out_specs=out_specs,
        check_vma=False,
    )
```
